256 devices in a mesh: rows: 256 (over x, y, z, core).
Axes of the slice: x: 4, y: 4, z: 8, core: 2. Of those that a mesh axis runs over, the one named last changes fastest.
Arguments:
- features: float32 [1048576, 64], P('rows'), may hold values from -6 to 6
- prev_factors: float32 [1048576, 384], P('rows'), may hold values from -0.15 to 0.15
- inv_scales: float32 [64], replicated, may hold values from 0.005 to 0.03
- noise: float32 [1], replicated, may hold values from 1 to 2
- pivot_owner: int32 [2, 64], replicated, may hold values from 0 to 255, as said below
- pivot_local: int32 [2, 64], replicated, may hold values from 0 to 4095, as said below
Outputs:
- new_factors: float32 [1048576, 128], P('rows')
- residual_diag: float32 [1048576], P('rows')
- trace: float32 [1], replicated
The draws below stay inside these ranges and needn't reach their ends.
Inputs may be any that keep to these rules, and one draw needn't show every extreme that they name: `pivot_owner`: device indices; low indices hold more pivots. `pivot_local`: all 128 pivot rows are distinct within their devices' rows, so all pivots are distinct.
All inputs are finite; a program needn't handle non-finite values.
Results may differ from the reference program's by a relative error of at most 0.00017.
Values sent between devices are 32-bit elements; how exact they have to be, the bound alone decides.
No kernel may reach another device: no remote copies, remote signals or barrier semaphores. Data moves between devices by JAX's collectives and lax.ppermute only.
A program may use at most 64 MiB of HBM per device.

```python
import math
import jax
import jax.numpy as jnp
from jax import lax

ROWS_DEV = 4096
FEAT = 64
PREV = 384
PANEL = 64
PANELS = 2
POINTS = 1048576
N_ROWS = 256


def draw_prev_factors(key, part):
    key = jax.random.fold_in(key, 31)
    values = jnp.clip(0.025 * jax.random.normal(key, (POINTS, PREV), jnp.float32), -0.15, 0.15)
    return values.astype(jnp.float32)


def draw_pivot_owner(key, part):
    key = jax.random.fold_in(key, 11)
    first, second = jax.random.split(key)
    left = jax.random.randint(first, (PANELS, PANEL), 0, N_ROWS)
    right = jax.random.randint(second, (PANELS, PANEL), 0, N_ROWS)
    owner = left * right // N_ROWS
    owner = owner.at[0, 0].set(N_ROWS - 1)
    owner = owner.at[1, 0].set(0)
    return owner.astype(jnp.int32)


def draw_pivot_local(key, part):
    key = jax.random.fold_in(key, 23)
    count = PANELS * PANEL
    shuffled = jax.random.permutation(key, ROWS_DEV - 2)[:count - 2] + 1
    ends = jnp.array([0, ROWS_DEV - 1], dtype=jnp.int32)
    places = jnp.concatenate([ends, shuffled.astype(jnp.int32)])
    return places.reshape(PANELS, PANEL).astype(jnp.int32)


def shard_levels(stream_key, shape, shards, least, high):
    level = 1.0
    for axis_at, blocks in shards:
        steps = jax.random.uniform(jax.random.fold_in(jax.random.fold_in(stream_key, 6), axis_at), (blocks,), jnp.float32, least / len(shards), high / len(shards))
        level = level * jnp.repeat(jnp.exp(steps), shape[axis_at] // blocks).reshape((-1,) + (1,) * (len(shape) - 1 - axis_at))
    return level


def scatter_about(rng, dims, deviation, limit, pieces=(), kind=jnp.bfloat16):
    entries = deviation * jax.random.normal(rng, dims, jnp.float32)
    if pieces:
        entries = entries * shard_levels(rng, dims, pieces, -0.22, 0.18)
    return jnp.clip(entries, -limit, limit).astype(kind)


def setup_inputs(seed: int = 0) -> dict:
    arg_keys = jax.random.split(jax.random.key(seed), 7)
    features = scatter_about(arg_keys[0], (POINTS, FEAT), 1.0, 6.0, ((0, 256),), jnp.float32)
    prev_factors = draw_prev_factors(jax.random.fold_in(arg_keys[6], 71), 0)
    inv_scales = jnp.clip(jnp.exp(jax.random.uniform(arg_keys[2], (FEAT,), jnp.float32, math.log(0.005), math.log(0.03))), 0.005, 0.03)
    noise = jnp.clip(jnp.exp(jax.random.uniform(arg_keys[3], (1,), jnp.float32, math.log(1.0), math.log(2.0))), 1.0, 2.0)
    pivot_owner = draw_pivot_owner(jax.random.fold_in(arg_keys[6], 71), 0)
    pivot_local = draw_pivot_local(jax.random.fold_in(arg_keys[6], 71), 0)
    return dict(features=features, prev_factors=prev_factors, inv_scales=inv_scales, noise=noise, pivot_owner=pivot_owner, pivot_local=pivot_local)


HIGH = lax.Precision.HIGHEST

def kernel_block(left, right, weights):
    scaled = left * weights
    cross = jnp.dot(scaled.astype(jnp.float32), right.T.astype(jnp.float32), precision=HIGH, preferred_element_type=jnp.float32)
    left_sq = jnp.sum(scaled * left, axis=1)
    right_sq = jnp.sum(right * right * weights, axis=1)
    return jnp.exp(-0.5 * (left_sq[:, None] + right_sq[None, :] - 2.0 * cross))

def reference(features, prev_factors, inv_scales, noise, pivot_owner, pivot_local):
    index = (pivot_owner * ROWS_DEV + pivot_local).astype(jnp.int32)
    total = features.shape[0]
    positions = jnp.arange(total, dtype=jnp.int32)
    blocks = []
    for panel in range(PANELS):
        idx = index[panel]
        piv_x = features[idx]
        piv_prev = prev_factors[idx]
        hit = (positions[:, None] == idx[None, :]).astype(jnp.float32)
        cols = kernel_block(features, piv_x, inv_scales) + noise[0] * hit
        cols = cols - jnp.dot(prev_factors.astype(jnp.float32), piv_prev.T.astype(jnp.float32), precision=HIGH, preferred_element_type=jnp.float32)
        pivot_block = kernel_block(piv_x, piv_x, inv_scales) + noise[0] * jnp.eye(PANEL, dtype=jnp.float32)
        pivot_block = pivot_block - jnp.dot(piv_prev.astype(jnp.float32), piv_prev.T.astype(jnp.float32), precision=HIGH, preferred_element_type=jnp.float32)
        for earlier in blocks:
            piv_e = earlier[idx]
            cols = cols - jnp.dot(earlier.astype(jnp.float32), piv_e.T.astype(jnp.float32), precision=HIGH, preferred_element_type=jnp.float32)
            pivot_block = pivot_block - jnp.dot(piv_e.astype(jnp.float32), piv_e.T.astype(jnp.float32), precision=HIGH, preferred_element_type=jnp.float32)
        lower = jnp.linalg.cholesky(pivot_block)
        fresh = lax.linalg.triangular_solve(lower, cols, left_side=False, lower=True, transpose_a=True)
        blocks.append(fresh)
    new_factors = jnp.concatenate(blocks, axis=1)
    residual_diag = 1.0 + noise[0] - jnp.sum(prev_factors * prev_factors, axis=1) - jnp.sum(new_factors * new_factors, axis=1)
    trace = jnp.sum(residual_diag).reshape(1)
    return (new_factors, residual_diag, trace)
```

```python
import functools

import jax
import jax.numpy as jnp
from jax import lax
from jax.experimental import pallas as pl
from jax.experimental.pallas import tpu as pltpu
from jax.sharding import PartitionSpec as P

F32 = jnp.float32
BF16 = jnp.bfloat16
HIGH = lax.Precision.HIGHEST
VMEM = pl.BlockSpec(memory_space=pltpu.VMEM)
SMEM = pl.BlockSpec(memory_space=pltpu.SMEM)
ANY = pl.BlockSpec(memory_space=pl.ANY)
NT = (((1,), (1,)), ((), ()))


def groups_of(total, fields):
    found = {}
    for index in range(total):
        key = index
        for stride, size in fields:
            key -= ((index // stride) % size) * stride
        found.setdefault(key, []).append(index)
    return list(found.values())


def exchange(blocks, groups):
    return lax.all_to_all(blocks, "rows", 0, 0, axis_index_groups=groups, tiled=True)


def pick_kernel(me_ref, owner_ref, place_ref, feat_ref, prev_ref, out_ref, feat_rows, prev_rows, sems):
    out_ref[...] = jnp.zeros_like(out_ref)
    pivots = owner_ref.shape[0]
    feat = feat_ref.shape[1]
    me = me_ref[0]

    def copies(pivot):
        base = pl.multiple_of((place_ref[pivot] // 8) * 8, 8)
        return (
            pltpu.make_async_copy(feat_ref.at[pl.ds(base, 8)], feat_rows.at[pivot], sems.at[0, pivot]),
            pltpu.make_async_copy(prev_ref.at[pl.ds(base, 8)], prev_rows.at[pivot], sems.at[1, pivot]),
        )

    def start(pivot, carry):
        @pl.when(owner_ref[pivot] == me)
        def _():
            for copy in copies(pivot):
                copy.start()

        return carry

    def finish(pivot, carry):
        @pl.when(owner_ref[pivot] == me)
        def _():
            for copy in copies(pivot):
                copy.wait()
            row = lax.rem(place_ref[pivot], 8)
            slot = pivot // 8
            inner = lax.rem(pivot, 8)
            x = feat_rows[pivot]
            fac = prev_rows[pivot]
            x = jnp.concatenate([x, jnp.zeros((8, 128 - feat), F32)], axis=1)
            for half, rows in ((0, jnp.concatenate([x, fac[:, :128]], axis=1)), (1, fac[:, 128:])):
                sub = lax.broadcasted_iota(jnp.int32, rows.shape, 0)
                only = jnp.sum(jnp.where(sub == row, rows, 0.0), axis=0, keepdims=True)
                out_ref[slot, half] = jnp.where(sub == inner, only, out_ref[slot, half])

        return carry

    lax.fori_loop(0, pivots, start, 0)
    lax.fori_loop(0, pivots, finish, 0)


def split2(value):
    high = value.astype(BF16)
    return high, (value - high.astype(F32)).astype(BF16)


def split3(value):
    high = value.astype(BF16)
    rest = value - high.astype(F32)
    mid = rest.astype(BF16)
    return high, mid, (rest - mid.astype(F32)).astype(BF16)


def invert_factor(block):
    size = block.shape[0]
    rows = [block[8 * at : 8 * at + 8] for at in range(size // 8)]
    lane = lax.broadcasted_iota(jnp.int32, (8, size), 1)
    sub = lax.broadcasted_iota(jnp.int32, (8, size), 0)
    for step in range(size - 1):
        home, inner = divmod(step, 8)
        here = lane == step
        pivot_row = rows[home][inner : inner + 1, :]
        inverse = 1.0 / pivot_row[:, step : step + 1]
        scaled = jnp.where(here[:1], 1.0, pivot_row) * inverse
        for at in range(home, size // 8):
            if at == home and inner == 7:
                continue
            now = rows[at]
            column = now[:, step : step + 1]
            if at == home:
                column = jnp.where(sub[:, :1] > inner, column, 0.0)
                kept = jnp.where(here & (sub > inner), 0.0, now)
            else:
                kept = jnp.where(here, 0.0, now)
            rows[at] = kept - column * scaled
    done = jnp.concatenate(rows, axis=0)
    row_id = lax.broadcasted_iota(jnp.int32, (size, size), 0)
    col_id = lax.broadcasted_iota(jnp.int32, (size, size), 1)
    diag = jnp.sum(jnp.where(row_id == col_id, done, 0.0), axis=1, keepdims=True)
    unit = jnp.where(row_id == col_id, 1.0, jnp.where(col_id < row_id, done, 0.0))
    return unit * lax.rsqrt(diag)


def panel_kernel(
    me_ref, noise_ref, owner_ref, place_ref, scales_ref, pivots_ref, feat_ref, prev_ref,
    new_ref, resid_ref, part_ref, cols_ref, squares_ref, *, tile,
):
    points, feat = feat_ref.shape
    width = prev_ref.shape[1]
    size = owner_ref.shape[1]
    noise = noise_ref[0]
    scales = scales_ref[...]
    low = pivots_ref[:, 0].reshape(size, 256)
    piv_x = low[:, :feat]
    piv_f = jnp.concatenate([low[:, 128:], pivots_ref[:, 1].reshape(size, 256)], axis=1)

    piv_s = piv_x * scales
    cross = lax.dot_general(piv_s, piv_x, NT, precision=HIGH, preferred_element_type=F32)
    squared = piv_s * piv_x
    left_sq = jnp.sum(squared, axis=1, keepdims=True)
    right_sq = lax.dot_general(
        jnp.ones((8, feat), F32), squared, NT, precision=HIGH, preferred_element_type=F32
    )[:1]
    row_id = lax.broadcasted_iota(jnp.int32, (size, size), 0)
    col_id = lax.broadcasted_iota(jnp.int32, (size, size), 1)
    block = jnp.exp(-0.5 * (left_sq + right_sq - 2.0 * cross))
    block = block + jnp.where(row_id == col_id, noise, 0.0)
    block = block - lax.dot_general(piv_f, piv_f, NT, precision=HIGH, preferred_element_type=F32)
    inverse = invert_factor(block)

    mine = jnp.where(owner_ref[...] == me_ref[0], place_ref[...], -1)
    fac_high, fac_low = split2(piv_f)
    fac_rhs = jnp.concatenate(
        [jnp.concatenate([fac_high, fac_high], axis=1), jnp.concatenate([fac_low, fac_low], axis=1)],
        axis=0,
    )
    x_high, x_mid, x_low = split3(piv_x)
    x_rhs = jnp.concatenate([x_high, x_mid], axis=0)

    def columns(at, carry):
        base = pl.multiple_of(at * tile, tile)
        here = pl.ds(base, tile)
        x = feat_ref[here, :]
        s = x * scales
        left = jnp.sum(s * x, axis=1, keepdims=True)
        s_high, s_mid, s_low = split3(s)
        two = lax.dot_general(s_high, x_rhs, NT, preferred_element_type=F32)
        two = two + lax.dot_general(s_mid, x_rhs, NT, preferred_element_type=F32)
        cross = two[:, :size] + two[:, size:]
        cross = cross + lax.dot_general(s_high, x_low, NT, preferred_element_type=F32)
        cross = cross + lax.dot_general(s_low, x_high, NT, preferred_element_type=F32)
        kern = jnp.exp(-0.5 * (left + right_sq - 2.0 * cross))
        ids = lax.broadcasted_iota(jnp.int32, (tile, size), 0) + base
        kern = kern + jnp.where(ids == mine, noise, 0.0)
        fac = prev_ref[here, :]
        high, low_part = split2(fac)
        both = lax.dot_general(
            jnp.concatenate([high, low_part], axis=1), fac_rhs, NT, preferred_element_type=F32
        )
        cols_ref[here, :] = kern - (both[:, :size] + both[:, size:])
        total = fac[:, :128] * fac[:, :128]
        for start in range(128, width, 128):
            total = total + fac[:, start : start + 128] * fac[:, start : start + 128]
        squares_ref[here, :] = total
        return carry

    lax.fori_loop(0, points // tile, columns, 0)

    inv_high, inv_low = split2(inverse)
    inv_rhs = jnp.concatenate(
        [jnp.concatenate([inv_high, inv_high], axis=1), jnp.concatenate([inv_low, inv_low], axis=1)],
        axis=0,
    )

    def finish(at, total):
        here = pl.ds(pl.multiple_of(at * tile, tile), tile)
        high, low_part = split2(cols_ref[here, :])
        both = lax.dot_general(
            jnp.concatenate([high, low_part], axis=1), inv_rhs, NT, preferred_element_type=F32
        )
        new = both[:, :size] + both[:, size:]
        new_ref[here, :] = new
        gone = squares_ref[here, :] + new * new
        for sub_at in range(tile // 128):
            flipped = gone[sub_at * 128 : (sub_at + 1) * 128, :].T
            row = 1.0 + noise - jnp.sum(flipped, axis=0, keepdims=True)
            resid_ref[pl.ds(at * (tile // 128) + sub_at, 1), :] = row
            total = total + row
        return total

    total = lax.fori_loop(0, points // tile, finish, jnp.zeros((1, 128), F32))
    part_ref[...] = jnp.broadcast_to(jnp.sum(total, axis=1, keepdims=True), part_ref.shape)


def local(devices, features, prev_factors, inv_scales, noise, pivot_owner, pivot_local):
    points, feat = features.shape
    width = prev_factors.shape[1]
    pivots = pivot_owner.size
    me = lax.axis_index("rows").astype(jnp.int32).reshape(1)
    owner = pivot_owner.reshape(pivots)
    place = pivot_local.reshape(pivots)
    layer = groups_of(devices, ((1, 2), (16, 16)))
    column = groups_of(devices, ((2, 8),))

    picked = pl.pallas_call(
        pick_kernel,
        out_shape=jax.ShapeDtypeStruct((16, 2, 8, 256), F32),
        in_specs=[SMEM, SMEM, SMEM, ANY, ANY],
        out_specs=VMEM,
        scratch_shapes=[
            pltpu.VMEM((pivots, 8, feat), F32),
            pltpu.VMEM((pivots, 8, width), F32),
            pltpu.SemaphoreType.DMA((2, pivots)),
        ],
        name="pick",
    )(me, owner, place, features, prev_factors)

    part = exchange(picked.reshape(32, 8, 256), layer).sum(0)
    part = exchange(jnp.broadcast_to(part[None], (8, 8, 256)), column).sum(0)
    rows = exchange(jnp.broadcast_to(part[None], (32, 8, 256)), layer)

    new_factors, resid, part = pl.pallas_call(
        functools.partial(panel_kernel, tile=256),
        out_shape=(
            jax.ShapeDtypeStruct((points, pivots), F32),
            jax.ShapeDtypeStruct((points // 128, 128), F32),
            jax.ShapeDtypeStruct((devices, 128), F32),
        ),
        in_specs=[SMEM, SMEM, VMEM, VMEM, VMEM, VMEM, VMEM, VMEM],
        out_specs=(VMEM, VMEM, VMEM),
        scratch_shapes=[pltpu.VMEM((points, pivots), F32), pltpu.VMEM((points, 128), F32)],
        compiler_params=pltpu.CompilerParams(vmem_limit_bytes=32 * 1024 * 1024),
        name="panel",
    )(
        me, noise, owner.reshape(1, pivots), place.reshape(1, pivots), inv_scales.reshape(1, feat),
        rows.reshape(16, 2, 8, 256), features, prev_factors,
    )
    sums = exchange(part.reshape(devices, 1, 128), None)
    trace = jnp.sum(sums[:, 0, 0]).reshape(1)
    return new_factors, resid.reshape(points), trace


def solution(mesh):
    placed = (P("rows", None), P("rows", None), P(), P(), P(), P())
    return jax.shard_map(
        functools.partial(local, mesh.shape["rows"]),
        mesh=mesh,
        in_specs=placed,
        out_specs=(P("rows", None), P("rows"), P()),
        check_vma=False,
    )
```

```python
import functools

import jax
import jax.numpy as jnp
from jax import lax
from jax.experimental import pallas as pl
from jax.experimental.pallas import tpu as pltpu
from jax.sharding import PartitionSpec as P

F32 = jnp.float32
BF16 = jnp.bfloat16
HIGH = lax.Precision.HIGHEST
VMEM = pl.BlockSpec(memory_space=pltpu.VMEM)
SMEM = pl.BlockSpec(memory_space=pltpu.SMEM)
ANY = pl.BlockSpec(memory_space=pl.ANY)
HBM = pl.BlockSpec(memory_space=pltpu.HBM)
NT = (((1,), (1,)), ((), ()))


def groups_of(total, fields):
    found = {}
    for index in range(total):
        key = index
        for stride, size in fields:
            key -= ((index // stride) % size) * stride
        found.setdefault(key, []).append(index)
    return list(found.values())


def exchange(blocks, groups):
    return lax.all_to_all(blocks, "rows", 0, 0, axis_index_groups=groups, tiled=True)


def pick_kernel(
    owner_hbm, place_hbm, feat_hbm, prev_hbm, out_ref, owner_ref, place_ref, feat_part, prev_part, found,
    table_sems, sems,
):
    tables = (
        pltpu.make_async_copy(owner_hbm, owner_ref, table_sems.at[0]),
        pltpu.make_async_copy(place_hbm, place_ref, table_sems.at[1]),
    )
    for copy in tables:
        copy.start()
    out_ref[...] = jnp.zeros_like(out_ref)
    feat_part[...] = jnp.zeros_like(feat_part)
    panels, panel = owner_ref.shape
    feat = feat_hbm.shape[0]
    slots = feat_part.shape[0]
    me = lax.axis_index("rows")
    for copy in tables:
        copy.wait()
    count = jnp.int32(0)
    for pivot in range(panels * panel):
        found[count] = pivot
        count = count + (owner_ref[pivot // panel, pivot % panel] == me).astype(jnp.int32)

    def place_of(at):
        pivot = found[at]
        return pivot, place_ref[pivot // panel, lax.rem(pivot, panel)]

    def copies(at, place):
        wide = pl.ds(pl.multiple_of((place // 128) * 128, 128), 128)
        rows = pl.ds(pl.multiple_of((place // 8) * 8, 8), 8)
        slot = lax.rem(at, slots)
        return (
            pltpu.make_async_copy(feat_hbm.at[:, wide], feat_part.at[slot], sems.at[0, slot]),
            pltpu.make_async_copy(prev_hbm.at[rows, :], prev_part.at[slot], sems.at[1, slot]),
        )

    def start(at, carry):
        for copy in copies(at, place_of(at)[1]):
            copy.start()
        return carry

    def land(at, carry):
        for copy in copies(at, place_of(at)[1]):
            copy.wait()
        return carry

    sub = lax.broadcasted_iota(jnp.int32, (8, 128), 0)
    lane = lax.broadcasted_iota(jnp.int32, (8, 128), 1)
    wide_sub = lax.broadcasted_iota(jnp.int32, (8, 256), 0)
    fac_sub = lax.broadcasted_iota(jnp.int32, prev_part.shape[1:], 0)

    def batch(at, carry):
        first = at * slots
        last = jnp.minimum(first + slots, count)
        lax.fori_loop(first, last, start, 0)
        lax.fori_loop(first, last, land, 0)
        homes, xs, facs = [], 0.0, []
        for slot in range(slots):
            used = first + slot < last
            pivot, place = place_of(jnp.where(used, first + slot, first))
            homes.append((pivot // 8, jnp.where(used, lax.rem(pivot, 8), -1)))
            only = jnp.where((sub == slot) & (lane == lax.rem(place, 128)), 1.0, 0.0)
            xs = xs + lax.dot_general(only, feat_part[slot], NT, precision=HIGH, preferred_element_type=F32)
            fac = jnp.where(fac_sub == lax.rem(place, 8), prev_part[slot], 0.0)
            facs.append(jnp.sum(fac, axis=0, keepdims=True))
        xs = jnp.concatenate([xs, jnp.zeros((slots, 128 - feat), F32)], axis=1)
        for slot, (home, inner) in enumerate(homes):
            here = wide_sub == inner
            left = jnp.concatenate([xs[slot : slot + 1], facs[slot][:, :128]], axis=1)
            out_ref[home, 0] = jnp.where(here, left, out_ref[home, 0])
            out_ref[home, 1] = jnp.where(here, facs[slot][:, 128:], out_ref[home, 1])
        return carry

    lax.fori_loop(0, (count + slots - 1) // slots, batch, 0)


def run_pick(pivot_owner, pivot_local, feat_t, prev):
    pivots = pivot_owner.size
    return pl.pallas_call(
        pick_kernel,
        out_shape=jax.ShapeDtypeStruct((16, 2, 8, 256), F32),
        in_specs=[HBM, HBM, HBM, HBM],
        out_specs=VMEM,
        scratch_shapes=[
            pltpu.SMEM(pivot_owner.shape, jnp.int32),
            pltpu.SMEM(pivot_local.shape, jnp.int32),
            pltpu.VMEM((8, feat_t.shape[0], 128), F32),
            pltpu.VMEM((8, 8, prev.shape[1]), F32),
            pltpu.SMEM((pivots + 1,), jnp.int32),
            pltpu.SemaphoreType.DMA((2,)),
            pltpu.SemaphoreType.DMA((2, 8)),
        ],
        compiler_params=pltpu.CompilerParams(vmem_limit_bytes=64 * 1024 * 1024),
        name="pick",
    )(pivot_owner, pivot_local, feat_t, prev)


def split2(value):
    high = value.astype(BF16)
    return high, (value - high.astype(F32)).astype(BF16)


def split3(value):
    high = value.astype(BF16)
    rest = value - high.astype(F32)
    mid = rest.astype(BF16)
    return high, mid, (rest - mid.astype(F32)).astype(BF16)


def factor_steps(block, result):
    size = block.shape[0]
    count = size // 8
    rows = [block[8 * at : 8 * at + 8] for at in range(count)]
    lane = lax.broadcasted_iota(jnp.int32, (8, size), 1)
    sub = lax.broadcasted_iota(jnp.int32, (8, size), 0)

    def spread(value, row):
        return jnp.broadcast_to(value[row : row + 1], (8, size))

    for home in range(count):
        first = 8 * home
        columns = [
            [jnp.broadcast_to(rows[at][:, first + k : first + k + 1], (8, size)) for at in range(home, count)]
            for k in range(8)
        ]
        inside = (lane >= first) & (lane < first + 8)
        top = jnp.where(inside, 0.0, rows[home])
        factors, pivots, diag = [], [], None
        for step in range(8):
            pivot = spread(columns[step][0], step)
            diag = pivot if diag is None else jnp.where(sub == step, pivot, diag)
            inverse = 1.0 / pivot
            factor = [value * inverse for value in columns[step]]
            factor[0] = jnp.where(sub > step, factor[0], 0.0)
            row = jnp.where(lane == first + step, 1.0, spread(top, step))
            if step < 7:
                top = top - factor[0] * row
                for k in range(step + 1, 8):
                    ahead = spread(columns[k][0], step)
                    columns[k] = [value - part * ahead for value, part in zip(columns[k], factor)]
            factors.append(factor)
            pivots.append(row)
        for at in range(home + 1, count):
            value = jnp.where(inside, 0.0, rows[at])
            for step in range(8):
                value = value - factors[step][at - home] * pivots[step]
            rows[at] = value
        unit = jnp.where(lane < sub + first, top, 0.0) + jnp.where(lane == sub + first, 1.0, 0.0)
        result.append(unit * lax.rsqrt(diag))
        yield


def stacked(value):
    high, low = split2(value)
    return jnp.concatenate(
        [jnp.concatenate([high, high], axis=1), jnp.concatenate([low, low], axis=1)], axis=0
    )


def panel_kernel(
    me_ref, noise_ref, owner_ref, place_ref, scales_ref, pivots_ref, feat_hbm, prev_hbm,
    new_hbm, resid_ref, part_ref,
    feat_ref, prev_ref, cols_ref, squares_ref, in_sems, out_sems, *, tile, chunk,
):
    feat, points = feat_ref.shape
    width = prev_ref.shape[1]
    size = owner_ref.shape[1]
    chunks = points // chunk
    noise = noise_ref[0]

    def incoming(at):
        here = pl.ds(at * chunk, chunk)
        return (
            pltpu.make_async_copy(feat_hbm.at[:, here], feat_ref.at[:, here], in_sems.at[0, at]),
            pltpu.make_async_copy(prev_hbm.at[here, :], prev_ref.at[here, :], in_sems.at[1, at]),
        )

    def outgoing(at):
        here = pl.ds(at * chunk, chunk)
        return pltpu.make_async_copy(cols_ref.at[here, :], new_hbm.at[here, :], out_sems.at[at])

    for at in range(chunks):
        for copy in incoming(at):
            copy.start()

    scales_row = scales_ref[...]
    scales_col = jnp.broadcast_to(scales_row, (8, feat)).T[:, :1]
    low = pivots_ref[:, 0].reshape(size, 256)
    piv_x = low[:, :feat]
    piv_f = jnp.concatenate([low[:, 128:], pivots_ref[:, 1].reshape(size, 256)], axis=1)
    piv_s = piv_x * scales_row
    piv_sq = jnp.sum(piv_s * piv_x, axis=1, keepdims=True)
    pad = jnp.zeros((size, 128 - feat), F32)
    lane = lax.broadcasted_iota(jnp.int32, (size, 128), 1)
    piv_left = jnp.concatenate([piv_x, pad], axis=1)
    piv_left = jnp.where(lane == feat, piv_sq, jnp.where(lane == feat + 1, 1.0, piv_left))
    piv_right = jnp.concatenate([piv_s, pad], axis=1)
    piv_right = jnp.where(lane == feat, -0.5, jnp.where(lane == feat + 1, -0.5 * piv_sq, piv_right))

    row_id = lax.broadcasted_iota(jnp.int32, (size, size), 0)
    col_id = lax.broadcasted_iota(jnp.int32, (size, size), 1)
    block = lax.dot_general(piv_left, piv_right, NT, precision=HIGH, preferred_element_type=F32)
    block = jnp.exp(block) + jnp.where(row_id == col_id, noise, 0.0)
    block = block - lax.dot_general(piv_f, piv_f, NT, precision=HIGH, preferred_element_type=F32)
    inverse_rows = []
    steps = factor_steps(block, inverse_rows)

    mine = jnp.where(owner_ref[...] == me_ref[0], place_ref[...], -1)
    fac_rhs = stacked(piv_f)
    x_high, x_mid, x_low = split3(piv_right)
    x_rhs = jnp.concatenate(
        [jnp.concatenate([x_high, x_high], axis=1), jnp.concatenate([x_mid, x_mid], axis=1)], axis=0
    )
    x_rest = jnp.concatenate([x_low, x_high], axis=1)
    sub = lax.broadcasted_iota(jnp.int32, (8, tile), 0)

    def columns(base):
        here = pl.ds(base, tile)
        xt = feat_ref[:, here]
        length = jnp.sum(xt * xt * scales_col, axis=0, keepdims=True)
        extra = jnp.where(sub == 0, length, jnp.where(sub == 1, 1.0, 0.0))
        left = jnp.concatenate([xt, extra, jnp.zeros((128 - feat - 8, tile), F32)], axis=0).T
        high, mid, low_part = split3(left)
        two = lax.dot_general(jnp.concatenate([high, mid], axis=1), x_rhs, NT, preferred_element_type=F32)
        rest = lax.dot_general(jnp.concatenate([high, low_part], axis=1), x_rest, NT, preferred_element_type=F32)
        kern = jnp.exp(two[:, :size] + (two[:, size:] + rest))
        ids = lax.broadcasted_iota(jnp.int32, (tile, size), 0) + base
        kern = kern + jnp.where(ids == mine, noise, 0.0)
        fac = prev_ref[here, :]
        high, low_part = split2(fac)
        both = lax.dot_general(
            jnp.concatenate([high, low_part], axis=1), fac_rhs, NT, preferred_element_type=F32
        )
        cols_ref[here, :] = kern - (both[:, :size] + both[:, size:])
        total = fac[:, :128] * fac[:, :128]
        for start in range(128, width, 128):
            total = total + fac[:, start : start + 128] * fac[:, start : start + 128]
        squares_ref[here, :] = total

    per_chunk = (size // 8) // chunks
    for at in range(chunks):
        for copy in incoming(at):
            copy.wait()
        for inner in range(chunk // tile):
            for _ in range(per_chunk * tile // chunk):
                next(steps)
            columns(at * chunk + inner * tile)
    for _ in steps:
        pass

    inv_rhs = stacked(jnp.concatenate(inverse_rows, axis=0))
    total = jnp.zeros((1, 128), F32)
    for at in range(chunks):
        for inner in range(chunk // tile):
            base = at * chunk + inner * tile
            here = pl.ds(base, tile)
            high, low_part = split2(cols_ref[here, :])
            both = lax.dot_general(
                jnp.concatenate([high, low_part], axis=1), inv_rhs, NT, preferred_element_type=F32
            )
            new = both[:, :size] + both[:, size:]
            cols_ref[here, :] = new
            gone = squares_ref[here, :] + new * new
            for sub_at in range(tile // 128):
                flipped = gone[sub_at * 128 : (sub_at + 1) * 128, :].T
                row = 1.0 + noise - jnp.sum(flipped, axis=0, keepdims=True)
                resid_ref[pl.ds(base // 128 + sub_at, 1), :] = row
                total = total + row
        outgoing(at).start()
    part_ref[...] = jnp.broadcast_to(jnp.sum(total, axis=1, keepdims=True), part_ref.shape)
    for at in range(chunks):
        outgoing(at).wait()


def run_panel(devices, me, noise, owner, place, scales, pivots, feat_t, prev):
    feat, points = feat_t.shape
    width = prev.shape[1]
    size = owner.shape[1]
    chunk = 512
    return pl.pallas_call(
        functools.partial(panel_kernel, tile=256, chunk=chunk),
        out_shape=(
            jax.ShapeDtypeStruct((points, size), F32),
            jax.ShapeDtypeStruct((points // 128, 128), F32),
            jax.ShapeDtypeStruct((devices, 128), F32),
        ),
        in_specs=[SMEM, SMEM, VMEM, VMEM, VMEM, VMEM, ANY, ANY],
        out_specs=(ANY, VMEM, VMEM),
        scratch_shapes=[
            pltpu.VMEM((feat, points), F32),
            pltpu.VMEM((points, width), F32),
            pltpu.VMEM((points, size), F32),
            pltpu.VMEM((points, 128), F32),
            pltpu.SemaphoreType.DMA((2, points // chunk)),
            pltpu.SemaphoreType.DMA((points // chunk,)),
        ],
        compiler_params=pltpu.CompilerParams(vmem_limit_bytes=64 * 1024 * 1024),
        name="panel",
    )(me, noise, owner, place, scales, pivots, feat_t, prev)


def local(devices, features, prev_factors, inv_scales, noise, pivot_owner, pivot_local):
    points, feat = features.shape
    pivots = pivot_owner.size
    feat_t = features.T
    me = lax.axis_index("rows").astype(jnp.int32).reshape(1)
    layer = groups_of(devices, ((1, 2), (16, 16)))
    column = groups_of(devices, ((2, 8),))

    picked = run_pick(pivot_owner, pivot_local, feat_t, prev_factors)
    part = exchange(picked.reshape(32, 8, 256), layer).sum(0)
    part = exchange(jnp.broadcast_to(part[None], (8, 8, 256)), column).sum(0)
    rows = exchange(jnp.broadcast_to(part[None], (32, 8, 256)), layer)
    new_factors, resid, part = run_panel(
        devices, me, noise, pivot_owner.reshape(1, pivots), pivot_local.reshape(1, pivots),
        inv_scales.reshape(1, feat), rows.reshape(16, 2, 8, 256), feat_t, prev_factors,
    )
    sums = exchange(part.reshape(devices, 1, 128), None)
    trace = jnp.sum(sums[:, 0, 0]).reshape(1)
    return new_factors, resid.reshape(points), trace


def solution(mesh):
    placed = (P("rows", None), P("rows", None), P(), P(), P(), P())
    return jax.shard_map(
        functools.partial(local, mesh.shape["rows"]),
        mesh=mesh,
        in_specs=placed,
        out_specs=(P("rows", None), P("rows"), P()),
        check_vma=False,
    )
```

```python
import functools

import jax
import jax.numpy as jnp
from jax import lax
from jax.experimental import pallas as pl
from jax.experimental.pallas import tpu as pltpu
from jax.sharding import PartitionSpec as P

F32 = jnp.float32
BF16 = jnp.bfloat16
HIGH = lax.Precision.HIGHEST
VMEM = pl.BlockSpec(memory_space=pltpu.VMEM)
SMEM = pl.BlockSpec(memory_space=pltpu.SMEM)
ANY = pl.BlockSpec(memory_space=pl.ANY)
HBM = pl.BlockSpec(memory_space=pltpu.HBM)
NT = (((1,), (1,)), ((), ()))
SMALL = 16 * 1024 * 1024
LAYERS = 8
RANKS = 8
SPOTS = 32
SPLITS = 4


def groups_of(total, fields):
    found = {}
    for index in range(total):
        key = index
        for stride, size in fields:
            key -= ((index // stride) % size) * stride
        found.setdefault(key, []).append(index)
    return list(found.values())


def exchange(blocks, groups):
    return lax.all_to_all(blocks, "rows", 0, 0, axis_index_groups=groups, tiled=True)


def pick_kernel(
    round_ref, owner_hbm, place_hbm, feat_hbm, prev_hbm, out_ref, owner_ref, place_ref, feat_part, prev_part,
    found, table_sems, sems,
):
    tables = (
        pltpu.make_async_copy(owner_hbm, owner_ref, table_sems.at[0]),
        pltpu.make_async_copy(place_hbm, place_ref, table_sems.at[1]),
    )
    for copy in tables:
        copy.start()
    feat_part[...] = jnp.zeros_like(feat_part)
    panels, panel = owner_ref.shape
    feat = feat_hbm.shape[0]
    me = lax.axis_index("rows")
    first = (round_ref[0] // SPLITS) * RANKS
    for copy in tables:
        copy.wait()
    count = jnp.int32(0)
    for pivot in range(panels * panel):
        found[count] = pivot
        count = count + (owner_ref[pivot // panel, pivot % panel] == me).astype(jnp.int32)
    count = jnp.clip(count - first, 0, RANKS)

    def place_of(at):
        pivot = found[first + at]
        return place_ref[pivot // panel, lax.rem(pivot, panel)]

    def copies(at):
        place = place_of(at)
        wide = pl.ds(pl.multiple_of((place // 128) * 128, 128), 128)
        rows = pl.ds(pl.multiple_of((place // 8) * 8, 8), 8)
        return (
            pltpu.make_async_copy(feat_hbm.at[:, wide], feat_part.at[at], sems.at[0, at]),
            pltpu.make_async_copy(prev_hbm.at[rows, :], prev_part.at[at], sems.at[1, at]),
        )

    def start(at, carry):
        for copy in copies(at):
            copy.start()
        return carry

    def land(at, carry):
        for copy in copies(at):
            copy.wait()
        return carry

    lax.fori_loop(0, count, start, 0)
    lax.fori_loop(0, count, land, 0)

    @pl.when(count > 0)
    def _():
        sub = lax.broadcasted_iota(jnp.int32, (RANKS, 128), 0)
        lane = lax.broadcasted_iota(jnp.int32, (RANKS, 128), 1)
        fac_sub = lax.broadcasted_iota(jnp.int32, prev_part.shape[1:], 0)
        xs, facs = 0.0, []
        for at in range(RANKS):
            used = at < count
            place = place_of(jnp.where(used, at, 0))
            only = jnp.where((sub == at) & (lane == lax.rem(place, 128)) & used, 1.0, 0.0)
            xs = xs + lax.dot_general(only, feat_part[at], NT, precision=HIGH, preferred_element_type=F32)
            fac = jnp.where((fac_sub == lax.rem(place, 8)) & used, prev_part[at], 0.0)
            facs.append(jnp.sum(fac, axis=0, keepdims=True))
        facs = jnp.concatenate(facs, axis=0)
        pad = jnp.zeros((RANKS, 128 - feat), F32)
        halves = (jnp.concatenate([xs, pad, facs[:, :128]], axis=1), facs[:, 128:])
        for at in range(out_ref.shape[0]):
            for half in range(2):
                out_ref[at, half] = halves[half]

    @pl.when(count == 0)
    def _():
        out_ref[...] = jnp.zeros_like(out_ref)


def run_pick(at_round, pivot_owner, pivot_local, feat_t, prev):
    return pl.pallas_call(
        pick_kernel,
        out_shape=jax.ShapeDtypeStruct((16, 2, RANKS, 256), F32),
        in_specs=[SMEM, HBM, HBM, HBM, HBM],
        out_specs=VMEM,
        scratch_shapes=[
            pltpu.SMEM(pivot_owner.shape, jnp.int32),
            pltpu.SMEM(pivot_local.shape, jnp.int32),
            pltpu.VMEM((RANKS, feat_t.shape[0], 128), F32),
            pltpu.VMEM((RANKS, 8, prev.shape[1]), F32),
            pltpu.SMEM((pivot_owner.size + 1,), jnp.int32),
            pltpu.SemaphoreType.DMA((2,)),
            pltpu.SemaphoreType.DMA((2, RANKS)),
        ],
        compiler_params=pltpu.CompilerParams(vmem_limit_bytes=64 * 1024 * 1024),
        name="pick",
    )(at_round, pivot_owner, pivot_local, feat_t, prev)


def table_kernel(
    round_ref, noise_ref, owner_ref, place_ref, scales_ref, pack_ref, pivots_ref, aux_ref, more_ref, rounds_ref
):
    panels, panel = owner_ref.shape
    size = panels * panel
    at_round = round_ref[0]
    window_now = (at_round // SPLITS).astype(F32)
    split_now = lax.rem(at_round, SPLITS).astype(F32)
    layer_now = lax.rem(lax.axis_index("rows") // 2, LAYERS).astype(F32)
    owner_row = jnp.concatenate([owner_ref[at : at + 1, :] for at in range(panels)], axis=1).astype(F32)
    place_row = jnp.concatenate([place_ref[at : at + 1, :] for at in range(panels)], axis=1).astype(F32)
    mine = jnp.where(owner_row == lax.axis_index("rows").astype(F32), place_row, -1.0)
    scales = jnp.concatenate([scales_ref[...], jnp.zeros_like(scales_ref)], axis=1)
    sub = lax.broadcasted_iota(jnp.int32, aux_ref.shape, 0)
    aux_ref[...] = jnp.where(sub == 0, mine, jnp.where(sub == 1, scales, noise_ref[0]))
    more_ref[...] = jnp.zeros_like(more_ref)
    owner_row = jnp.broadcast_to(owner_row, (size, size))
    owner_col = owner_row.T
    row_id = lax.broadcasted_iota(jnp.int32, (size, size), 0)
    col_id = lax.broadcasted_iota(jnp.int32, (size, size), 1)
    earlier = col_id < row_id

    def whole(value, unit):
        return jnp.floor(value * (1.0 / unit))

    def rest(value, unit):
        return value - unit * whole(value, unit)

    def ranks(same):
        found = jnp.sum(jnp.where(same & earlier, 1.0, 0.0), axis=1, keepdims=True)
        return jnp.broadcast_to(found, (size, size))

    rank = ranks(owner_row == owner_col)
    window = whole(rank, RANKS)
    layer_row = rest(whole(owner_row, 2), LAYERS)
    layer_col = rest(whole(owner_col, 2), LAYERS)
    spot = ranks((layer_row == layer_col) & (window == window.T))
    split = whole(spot, SPOTS)
    spot = rest(spot, SPOTS)
    active = (window == window_now) & (split == split_now)
    rounds_ref[0] = jnp.max(window * SPLITS + split).astype(jnp.int32) + 1

    wide = lax.broadcasted_iota(jnp.int32, (size, LAYERS * SPOTS), 1).astype(F32)
    both = lambda value: jnp.concatenate([value, value], axis=1)
    goal = both(jnp.where(active, layer_col * SPOTS + spot, -1.0))
    pivots_ref[...] = jnp.where(wide == goal, 1.0, 0.0)
    origin = (whole(owner_col, 2 * LAYERS) * 2 + rest(owner_col, 2)) * RANKS + rest(rank, RANKS)
    origin = jnp.where(wide == both(origin), 1.0, 0.0).astype(BF16)
    spot_row = jnp.where(active & (layer_col == layer_now), spot, -1.0).T[:SPOTS]
    target = lax.broadcasted_iota(jnp.int32, (SPOTS, size), 0).astype(F32)
    target = jnp.where(spot_row == target, 1.0, 0.0).astype(BF16)
    pack_ref[...] = jnp.dot(target, origin, preferred_element_type=F32)


def run_table(at_round, noise, pivot_owner, pivot_local, scales):
    size = pivot_owner.size
    return pl.pallas_call(
        table_kernel,
        out_shape=(
            jax.ShapeDtypeStruct((SPOTS, 32 * RANKS), F32),
            jax.ShapeDtypeStruct((size, LAYERS * SPOTS), F32),
            jax.ShapeDtypeStruct((8, size), F32),
            jax.ShapeDtypeStruct((size, 512), F32),
            jax.ShapeDtypeStruct((1,), jnp.int32),
        ),
        in_specs=[SMEM, SMEM, VMEM, VMEM, VMEM],
        out_specs=(VMEM, VMEM, VMEM, VMEM, SMEM),
        compiler_params=pltpu.CompilerParams(vmem_limit_bytes=SMALL),
        name="table",
    )(at_round, noise, pivot_owner, pivot_local, scales)


def pack_kernel(table_ref, rows_ref, out_ref):
    packed = jnp.dot(table_ref[...], rows_ref[...], precision=HIGH, preferred_element_type=F32)
    for at in range(out_ref.shape[0]):
        out_ref[at] = packed


def run_pack(table, rows):
    return pl.pallas_call(
        pack_kernel,
        out_shape=jax.ShapeDtypeStruct((LAYERS, SPOTS, 256), F32),
        in_specs=[VMEM, VMEM],
        out_specs=VMEM,
        compiler_params=pltpu.CompilerParams(vmem_limit_bytes=SMALL),
        name="pack",
    )(table, rows)


def unpack(table, near, far, core):
    first = jnp.where(core == 0, near, far).reshape(LAYERS * SPOTS, 256)
    second = jnp.where(core == 0, far, near).reshape(LAYERS * SPOTS, 256)
    return jnp.concatenate(
        [
            jnp.dot(table, first, precision=HIGH, preferred_element_type=F32),
            jnp.dot(table, second, precision=HIGH, preferred_element_type=F32),
        ],
        axis=1,
    )


def split2(value):
    high = value.astype(BF16)
    return high, (value - high.astype(F32)).astype(BF16)


def split3(value):
    high = value.astype(BF16)
    rest = value - high.astype(F32)
    mid = rest.astype(BF16)
    return high, mid, (rest - mid.astype(F32)).astype(BF16)


def factor_steps(block, result):
    size = block.shape[0]
    count = size // 8
    rows = [block[8 * at : 8 * at + 8] for at in range(count)]
    lane = lax.broadcasted_iota(jnp.int32, (8, size), 1)
    sub = lax.broadcasted_iota(jnp.int32, (8, size), 0)

    def spread(value, row):
        return jnp.broadcast_to(value[row : row + 1], (8, size))

    for home in range(count):
        first = 8 * home
        columns = [
            [jnp.broadcast_to(rows[at][:, first + k : first + k + 1], (8, size)) for at in range(home, count)]
            for k in range(8)
        ]
        inside = (lane >= first) & (lane < first + 8)
        top = jnp.where(inside, 0.0, rows[home])
        factors, pivots, diag = [], [], None
        for step in range(8):
            pivot = spread(columns[step][0], step)
            diag = pivot if diag is None else jnp.where(sub == step, pivot, diag)
            inverse = 1.0 / pivot
            factor = [value * inverse for value in columns[step]]
            factor[0] = jnp.where(sub > step, factor[0], 0.0)
            row = jnp.where(lane == first + step, 1.0, spread(top, step))
            if step < 7:
                top = top - factor[0] * row
                for k in range(step + 1, 8):
                    ahead = spread(columns[k][0], step)
                    columns[k] = [value - part * ahead for value, part in zip(columns[k], factor)]
            factors.append(factor)
            pivots.append(row)
        for at in range(home + 1, count):
            value = jnp.where(inside, 0.0, rows[at])
            for step in range(8):
                value = value - factors[step][at - home] * pivots[step]
            rows[at] = value
        unit = jnp.where(lane < sub + first, top, 0.0) + jnp.where(lane == sub + first, 1.0, 0.0)
        result.append(unit * lax.rsqrt(diag))
        yield


def stacked(value):
    high, low = split2(value)
    return jnp.concatenate(
        [jnp.concatenate([high, high], axis=1), jnp.concatenate([low, low], axis=1)], axis=0
    )


def panel_kernel(
    rounds_ref, aux_hbm, table_hbm, near_hbm, far_hbm, more_hbm, feat_hbm, prev_hbm,
    new_hbm, resid_ref, part_ref,
    aux_ref, table_ref, near_ref, far_ref, more_ref, feat_ref, prev_ref, cols_ref, squares_ref,
    first_sems, in_sems, out_sems, *, tile, chunk,
):
    feat, points = feat_ref.shape
    width = prev_ref.shape[1]
    size = aux_ref.shape[1]
    chunks = points // chunk

    pairs = ((near_hbm, near_ref), (far_hbm, far_ref), (table_hbm, table_ref), (aux_hbm, aux_ref))
    first_copies = [
        pltpu.make_async_copy(source, target, first_sems.at[at]) for at, (source, target) in enumerate(pairs)
    ]
    for copy in first_copies:
        copy.start()

    def incoming(at):
        here = pl.ds(at * chunk, chunk)
        return (
            pltpu.make_async_copy(feat_hbm.at[:, here], feat_ref.at[:, here], in_sems.at[0, at]),
            pltpu.make_async_copy(prev_hbm.at[here, :], prev_ref.at[here, :], in_sems.at[1, at]),
        )

    def outgoing(at):
        here = pl.ds(at * chunk, chunk)
        return pltpu.make_async_copy(cols_ref.at[here, :], new_hbm.at[here, :], out_sems.at[at])

    @pl.when(rounds_ref[0] > 1)
    def _():
        copy = pltpu.make_async_copy(more_hbm, more_ref, first_sems.at[len(pairs)])
        copy.start()
        copy.wait()

    @pl.when(rounds_ref[0] <= 1)
    def _():
        more_ref[...] = jnp.zeros_like(more_ref)

    for copy in first_copies:
        copy.wait()
    for at in range(chunks):
        for copy in incoming(at):
            copy.start()

    mine = aux_ref[0:1, :]
    scales_row = aux_ref[1:2, :feat]
    noise = aux_ref[2:3, :]
    scales_col = jnp.broadcast_to(aux_ref[1:2, :], (8, size)).T[:feat, :1]
    core = lax.rem(lax.axis_index("rows"), 2)
    rows = unpack(table_ref[...], near_ref[...], far_ref[...], core) + more_ref[...]
    piv_x = rows[:, :feat]
    piv_f = rows[:, 128:]
    piv_s = piv_x * scales_row
    piv_sq = jnp.sum(piv_s * piv_x, axis=1, keepdims=True)
    pad = jnp.zeros((size, 128 - feat), F32)
    lane = lax.broadcasted_iota(jnp.int32, (size, 128), 1)
    piv_left = jnp.concatenate([piv_x, pad], axis=1)
    piv_left = jnp.where(lane == feat, piv_sq, jnp.where(lane == feat + 1, 1.0, piv_left))
    piv_right = jnp.concatenate([piv_s, pad], axis=1)
    piv_right = jnp.where(lane == feat, -0.5, jnp.where(lane == feat + 1, -0.5 * piv_sq, piv_right))

    row_id = lax.broadcasted_iota(jnp.int32, (size, size), 0)
    col_id = lax.broadcasted_iota(jnp.int32, (size, size), 1)
    block = lax.dot_general(piv_left, piv_right, NT, precision=HIGH, preferred_element_type=F32)
    block = jnp.exp(block) + jnp.where(row_id == col_id, noise, 0.0)
    block = block - lax.dot_general(piv_f, piv_f, NT, precision=HIGH, preferred_element_type=F32)
    inverse_rows = []
    steps = factor_steps(block, inverse_rows)

    fac_rhs = stacked(piv_f)
    x_high, x_mid, x_low = split3(piv_right)
    x_rhs = jnp.concatenate(
        [jnp.concatenate([x_high, x_high], axis=1), jnp.concatenate([x_mid, x_mid], axis=1)], axis=0
    )
    x_rest = jnp.concatenate([x_low, x_high], axis=1)
    sub = lax.broadcasted_iota(jnp.int32, (8, tile), 0)
    ids = lax.broadcasted_iota(jnp.int32, (tile, size), 0).astype(F32)

    def columns(base):
        here = pl.ds(base, tile)
        xt = feat_ref[:, here]
        length = jnp.sum(xt * xt * scales_col, axis=0, keepdims=True)
        extra = jnp.where(sub == 0, length, jnp.where(sub == 1, 1.0, 0.0))
        left = jnp.concatenate([xt, extra, jnp.zeros((128 - feat - 8, tile), F32)], axis=0).T
        high, mid, low_part = split3(left)
        two = lax.dot_general(jnp.concatenate([high, mid], axis=1), x_rhs, NT, preferred_element_type=F32)
        rest = lax.dot_general(jnp.concatenate([high, low_part], axis=1), x_rest, NT, preferred_element_type=F32)
        kern = jnp.exp(two[:, :size] + (two[:, size:] + rest))
        kern = kern + jnp.where(ids == mine - base, noise, 0.0)
        fac = prev_ref[here, :]
        high, low_part = split2(fac)
        both = lax.dot_general(
            jnp.concatenate([high, low_part], axis=1), fac_rhs, NT, preferred_element_type=F32
        )
        cols_ref[here, :] = kern - (both[:, :size] + both[:, size:])
        total = fac[:, :128] * fac[:, :128]
        for start in range(128, width, 128):
            total = total + fac[:, start : start + 128] * fac[:, start : start + 128]
        squares_ref[here, :] = total

    per_chunk = (size // 8) // chunks
    for at in range(chunks):
        for copy in incoming(at):
            copy.wait()
        for inner in range(chunk // tile):
            for _ in range(per_chunk * tile // chunk):
                next(steps)
            columns(at * chunk + inner * tile)
    for _ in steps:
        pass

    inv_rhs = stacked(jnp.concatenate(inverse_rows, axis=0))
    total = jnp.zeros((1, 128), F32)
    for at in range(chunks):
        for inner in range(chunk // tile):
            base = at * chunk + inner * tile
            here = pl.ds(base, tile)
            high, low_part = split2(cols_ref[here, :])
            both = lax.dot_general(
                jnp.concatenate([high, low_part], axis=1), inv_rhs, NT, preferred_element_type=F32
            )
            new = both[:, :size] + both[:, size:]
            cols_ref[here, :] = new
            gone = squares_ref[here, :] + new * new
            for sub_at in range(tile // 128):
                flipped = gone[sub_at * 128 : (sub_at + 1) * 128, :].T
                row = 1.0 + noise - jnp.sum(flipped, axis=0, keepdims=True)
                resid_ref[pl.ds(base // 128 + sub_at, 1), :] = row
                total = total + row
        outgoing(at).start()
    part_ref[...] = jnp.broadcast_to(jnp.sum(total, axis=1, keepdims=True), part_ref.shape)
    for at in range(chunks):
        outgoing(at).wait()


def run_panel(devices, rounds, aux, table, near, far, more, feat_t, prev):
    feat, points = feat_t.shape
    width = prev.shape[1]
    size = aux.shape[1]
    chunk = 512
    return pl.pallas_call(
        functools.partial(panel_kernel, tile=256, chunk=chunk),
        out_shape=(
            jax.ShapeDtypeStruct((points, size), F32),
            jax.ShapeDtypeStruct((points // 128, 128), F32),
            jax.ShapeDtypeStruct((devices, 128), F32),
        ),
        in_specs=[SMEM] + [ANY] * 7,
        out_specs=(ANY, VMEM, VMEM),
        scratch_shapes=[
            pltpu.VMEM(aux.shape, F32),
            pltpu.VMEM(table.shape, F32),
            pltpu.VMEM(near.shape, F32),
            pltpu.VMEM(far.shape, F32),
            pltpu.VMEM(more.shape, F32),
            pltpu.VMEM((feat, points), F32),
            pltpu.VMEM((points, width), F32),
            pltpu.VMEM((points, size), F32),
            pltpu.VMEM((points, 128), F32),
            pltpu.SemaphoreType.DMA((5,)),
            pltpu.SemaphoreType.DMA((2, points // chunk)),
            pltpu.SemaphoreType.DMA((points // chunk,)),
        ],
        compiler_params=pltpu.CompilerParams(vmem_limit_bytes=64 * 1024 * 1024),
        name="panel",
    )(rounds, aux, table, near, far, more, feat_t, prev)


def local(devices, features, prev_factors, inv_scales, noise, pivot_owner, pivot_local):
    points, feat = features.shape
    feat_t = features.T
    layer = groups_of(devices, ((1, 2), (16, 16)))
    column = groups_of(devices, ((2, LAYERS),))
    cores = [(at, at ^ 1) for at in range(devices)]

    def fetch(at_round):
        picked = run_pick(at_round, pivot_owner, pivot_local, feat_t, prev_factors)
        landed = exchange(picked.reshape(32, RANKS, 256), layer)
        pack_table, table, aux, more, rounds = run_table(
            at_round, noise, pivot_owner, pivot_local, inv_scales.reshape(1, feat)
        )
        packed = run_pack(pack_table, landed.reshape(32 * RANKS, 256))
        near = exchange(packed, column)
        return table, near, lax.ppermute(near, "rows", cores), aux, more, rounds

    def again(carry):
        at_round, more = carry
        table, near, far, *_ = fetch(at_round.reshape(1))
        return at_round + 1, more + unpack(table, near, far, lax.rem(lax.axis_index("rows"), 2))

    table, near, far, aux, more, rounds = fetch(jnp.zeros((1,), jnp.int32))
    _, more = lax.while_loop(lambda carry: carry[0] < rounds[0], again, (jnp.int32(1), more))
    new_factors, resid, part = run_panel(devices, rounds, aux, table, near, far, more, feat_t, prev_factors)
    sums = exchange(part.reshape(devices, 1, 128), None)
    trace = jnp.sum(sums[:, 0, 0]).reshape(1)
    return new_factors, resid.reshape(points), trace


def solution(mesh):
    placed = (P("rows", None), P("rows", None), P(), P(), P(), P())
    return jax.shard_map(
        functools.partial(local, mesh.shape["rows"]),
        mesh=mesh,
        in_specs=placed,
        out_specs=(P("rows", None), P("rows"), P()),
        check_vma=False,
    )
```

```python
import functools

import jax
import jax.numpy as jnp
from jax import lax
from jax.experimental import pallas as pl
from jax.experimental.pallas import tpu as pltpu
from jax.sharding import PartitionSpec as P

F32 = jnp.float32
BF16 = jnp.bfloat16
HIGH = lax.Precision.HIGHEST
VMEM = pl.BlockSpec(memory_space=pltpu.VMEM)
SMEM = pl.BlockSpec(memory_space=pltpu.SMEM)
ANY = pl.BlockSpec(memory_space=pl.ANY)
HBM = pl.BlockSpec(memory_space=pltpu.HBM)
NT = (((1,), (1,)), ((), ()))
SMALL = 16 * 1024 * 1024
PANEL = 64 * 1024 * 1024 - 840 * 1024
LAYERS = 8
RANKS = 8
SPOTS = 32
SPLITS = 4


def groups_of(total, fields):
    found = {}
    for index in range(total):
        key = index
        for stride, size in fields:
            key -= ((index // stride) % size) * stride
        found.setdefault(key, []).append(index)
    return list(found.values())


def exchange(blocks, groups):
    return lax.all_to_all(blocks, "rows", 0, 0, axis_index_groups=groups, tiled=True)


def pick_kernel(
    round_ref, owner_hbm, place_hbm, feat_hbm, prev_hbm, out_ref, owner_ref, place_ref, feat_part, prev_part,
    found, table_sems, sems,
):
    tables = (
        pltpu.make_async_copy(owner_hbm, owner_ref, table_sems.at[0]),
        pltpu.make_async_copy(place_hbm, place_ref, table_sems.at[1]),
    )
    for copy in tables:
        copy.start()
    feat_part[...] = jnp.zeros_like(feat_part)
    panels, panel = owner_ref.shape
    feat = feat_hbm.shape[0]
    me = lax.axis_index("rows")
    first = (round_ref[0] // SPLITS) * RANKS
    for copy in tables:
        copy.wait()
    count = jnp.int32(0)
    for pivot in range(panels * panel):
        found[count] = pivot
        count = count + (owner_ref[pivot // panel, pivot % panel] == me).astype(jnp.int32)
    count = jnp.clip(count - first, 0, RANKS)

    def place_of(at):
        pivot = found[first + at]
        return place_ref[pivot // panel, lax.rem(pivot, panel)]

    def copies(at):
        place = place_of(at)
        wide = pl.ds(pl.multiple_of((place // 128) * 128, 128), 128)
        rows = pl.ds(pl.multiple_of((place // 8) * 8, 8), 8)
        return (
            pltpu.make_async_copy(feat_hbm.at[:, wide], feat_part.at[at], sems.at[0, at]),
            pltpu.make_async_copy(prev_hbm.at[rows, :], prev_part.at[at], sems.at[1, at]),
        )

    def start(at, carry):
        for copy in copies(at):
            copy.start()
        return carry

    def land(at, carry):
        for copy in copies(at):
            copy.wait()
        return carry

    lax.fori_loop(0, count, start, 0)
    lax.fori_loop(0, count, land, 0)

    @pl.when(count > 0)
    def _():
        lane = lax.broadcasted_iota(jnp.int32, (feat, 128), 1)
        fac_sub = lax.broadcasted_iota(jnp.int32, prev_part.shape[1:], 0)
        xs, facs = jnp.zeros((feat, 128), F32), []
        for at in range(RANKS):
            used = at < count
            place = place_of(jnp.where(used, at, 0))
            x = jnp.where((lane == lax.rem(place, 128)) & used, feat_part[at], 0.0)
            xs = jnp.where(lane == at, jnp.sum(x, axis=1, keepdims=True), xs)
            fac = jnp.where((fac_sub == lax.rem(place, 8)) & used, prev_part[at], 0.0)
            facs.append(jnp.sum(fac, axis=0, keepdims=True))
        xs = jnp.concatenate([xs, jnp.zeros((128 - feat, 128), F32)], axis=0).T[:RANKS]
        facs = jnp.concatenate(facs, axis=0)
        halves = (jnp.concatenate([xs, facs[:, :128]], axis=1), facs[:, 128:])
        for at in range(out_ref.shape[0]):
            for half in range(2):
                out_ref[at, half] = halves[half]

    @pl.when(count == 0)
    def _():
        out_ref[...] = jnp.zeros_like(out_ref)


def run_pick(at_round, pivot_owner, pivot_local, feat_t, prev):
    return pl.pallas_call(
        pick_kernel,
        out_shape=jax.ShapeDtypeStruct((16, 2, RANKS, 256), F32),
        in_specs=[SMEM, HBM, HBM, HBM, HBM],
        out_specs=VMEM,
        scratch_shapes=[
            pltpu.SMEM(pivot_owner.shape, jnp.int32),
            pltpu.SMEM(pivot_local.shape, jnp.int32),
            pltpu.VMEM((RANKS, feat_t.shape[0], 128), F32),
            pltpu.VMEM((RANKS, 8, prev.shape[1]), F32),
            pltpu.SMEM((pivot_owner.size + 1,), jnp.int32),
            pltpu.SemaphoreType.DMA((2,)),
            pltpu.SemaphoreType.DMA((2, RANKS)),
        ],
        compiler_params=pltpu.CompilerParams(vmem_limit_bytes=64 * 1024 * 1024),
        name="pick",
    )(at_round, pivot_owner, pivot_local, feat_t, prev)


def table_kernel(
    round_ref, noise_ref, owner_ref, place_ref, scales_ref, pack_ref, pivots_ref, aux_ref, more_ref, rounds_ref
):
    panels, panel = owner_ref.shape
    size = panels * panel
    at_round = round_ref[0]
    window_now = (at_round // SPLITS).astype(F32)
    split_now = lax.rem(at_round, SPLITS).astype(F32)
    layer_now = lax.rem(lax.axis_index("rows") // 2, LAYERS).astype(F32)
    owner_row = jnp.concatenate([owner_ref[at : at + 1, :] for at in range(panels)], axis=1).astype(F32)
    place_row = jnp.concatenate([place_ref[at : at + 1, :] for at in range(panels)], axis=1).astype(F32)
    mine = jnp.where(owner_row == lax.axis_index("rows").astype(F32), place_row, -1.0)
    scales = jnp.concatenate([scales_ref[...], jnp.zeros_like(scales_ref)], axis=1)
    sub = lax.broadcasted_iota(jnp.int32, aux_ref.shape, 0)
    aux_ref[...] = jnp.where(sub == 0, mine, jnp.where(sub == 1, scales, noise_ref[0]))
    more_ref[...] = jnp.zeros_like(more_ref)
    owner_row = jnp.broadcast_to(owner_row, (size, size))
    owner_col = owner_row.T
    row_id = lax.broadcasted_iota(jnp.int32, (size, size), 0)
    col_id = lax.broadcasted_iota(jnp.int32, (size, size), 1)
    earlier = col_id < row_id

    def whole(value, unit):
        return jnp.floor(value * (1.0 / unit))

    def rest(value, unit):
        return value - unit * whole(value, unit)

    def ranks(same):
        found = jnp.sum(jnp.where(same & earlier, 1.0, 0.0), axis=1, keepdims=True)
        return jnp.broadcast_to(found, (size, size))

    rank = ranks(owner_row == owner_col)
    window = whole(rank, RANKS)
    layer_row = rest(whole(owner_row, 2), LAYERS)
    layer_col = rest(whole(owner_col, 2), LAYERS)
    spot = ranks((layer_row == layer_col) & (window == window.T))
    split = whole(spot, SPOTS)
    spot = rest(spot, SPOTS)
    active = (window == window_now) & (split == split_now)
    rounds_ref[0] = jnp.max(window * SPLITS + split).astype(jnp.int32) + 1

    wide = lax.broadcasted_iota(jnp.int32, (size, LAYERS * SPOTS), 1).astype(F32)
    both = lambda value: jnp.concatenate([value, value], axis=1)
    goal = both(jnp.where(active, layer_col * SPOTS + spot, -1.0))
    pivots_ref[...] = jnp.where(wide == goal, 1.0, 0.0)
    origin = (whole(owner_col, 2 * LAYERS) * 2 + rest(owner_col, 2)) * RANKS + rest(rank, RANKS)
    origin = jnp.where(wide == both(origin), 1.0, 0.0).astype(BF16)
    spot_row = jnp.where(active & (layer_col == layer_now), spot, -1.0).T[:SPOTS]
    target = lax.broadcasted_iota(jnp.int32, (SPOTS, size), 0).astype(F32)
    target = jnp.where(spot_row == target, 1.0, 0.0).astype(BF16)
    pack_ref[...] = jnp.dot(target, origin, preferred_element_type=F32)


def run_table(at_round, noise, pivot_owner, pivot_local, scales):
    size = pivot_owner.size
    return pl.pallas_call(
        table_kernel,
        out_shape=(
            jax.ShapeDtypeStruct((SPOTS, 32 * RANKS), F32),
            jax.ShapeDtypeStruct((size, LAYERS * SPOTS), F32),
            jax.ShapeDtypeStruct((8, size), F32),
            jax.ShapeDtypeStruct((size, 512), F32),
            jax.ShapeDtypeStruct((1,), jnp.int32),
        ),
        in_specs=[SMEM, SMEM, VMEM, VMEM, VMEM],
        out_specs=(VMEM, VMEM, VMEM, VMEM, SMEM),
        compiler_params=pltpu.CompilerParams(vmem_limit_bytes=SMALL),
        name="table",
    )(at_round, noise, pivot_owner, pivot_local, scales)


def pack_kernel(table_ref, rows_ref, out_ref):
    packed = pick_rows(table_ref[...], rows_ref[...])
    for at in range(out_ref.shape[0]):
        out_ref[at] = packed


def run_pack(table, rows):
    return pl.pallas_call(
        pack_kernel,
        out_shape=jax.ShapeDtypeStruct((LAYERS, SPOTS, 256), F32),
        in_specs=[VMEM, VMEM],
        out_specs=VMEM,
        compiler_params=pltpu.CompilerParams(vmem_limit_bytes=SMALL),
        name="pack",
    )(table, rows)


def unpack(table, near, far, core):
    first = jnp.where(core == 0, near, far).reshape(LAYERS * SPOTS, 256)
    second = jnp.where(core == 0, far, near).reshape(LAYERS * SPOTS, 256)
    return pick_rows(table, jnp.concatenate([first, second], axis=1))


def pick_rows(table, rows):
    table = table.astype(BF16)
    high, mid, low = [jnp.dot(table, part, preferred_element_type=F32) for part in split3(rows)]
    return high + mid + low


def split2(value):
    high = value.astype(BF16)
    return high, (value - high.astype(F32)).astype(BF16)


def split3(value):
    high = value.astype(BF16)
    rest = value - high.astype(F32)
    mid = rest.astype(BF16)
    return high, mid, (rest - mid.astype(F32)).astype(BF16)


def factor_steps(block, result):
    size = block.shape[0]
    count = size // 8
    rows = [block[8 * at : 8 * at + 8] for at in range(count)]
    lane = lax.broadcasted_iota(jnp.int32, (8, size), 1)
    sub = lax.broadcasted_iota(jnp.int32, (8, size), 0)

    def spread_row(value, row):
        return jnp.broadcast_to(value[row : row + 1], (8, size))

    def spread_columns(value, first):
        return [jnp.broadcast_to(value[:, first + k : first + k + 1], (8, size)) for k in range(8)]

    diagonal = spread_columns(rows[0], 0)
    for home in range(count):
        first = 8 * home
        more = home + 1 < count
        inside = (lane >= first) & (lane < first + 8)
        top = jnp.where(inside, 0.0, rows[home])
        pivots, inverses, ahead, pivot_col = [], [], {}, None
        if more:
            below = spread_columns(rows[home + 1], first)
            coming = spread_columns(rows[home + 1], first + 8)
            below_factors = []
        for step in range(8):
            pivot = spread_row(diagonal[step], step)
            pivot_col = pivot if pivot_col is None else jnp.where(sub == step, pivot, pivot_col)
            inverse = 1.0 / pivot
            inverses.append(inverse)
            factor = jnp.where(sub > step, diagonal[step] * inverse, 0.0)
            for k in range(step + 1, 8):
                ahead[k, step] = spread_row(diagonal[k], step)
                diagonal[k] = diagonal[k] - factor * ahead[k, step]
            if more:
                part = below[step] * inverse
                below_factors.append(part)
                for k in range(step + 1, 8):
                    below[k] = below[k] - part * ahead[k, step]
                for k in range(8):
                    coming[k] = coming[k] - part * spread_row(below[step], k)
            row = jnp.where(lane == first + step, 1.0, spread_row(top, step))
            pivots.append(row)
            if step < 7:
                top = top - factor * row
        for at in range(home + 1, count):
            if at == home + 1:
                factors = below_factors
            else:
                columns = spread_columns(rows[at], first)
                factors = []
                for step in range(8):
                    part = columns[step] * inverses[step]
                    factors.append(part)
                    for k in range(step + 1, 8):
                        columns[k] = columns[k] - part * ahead[k, step]
            value = jnp.where(inside, 0.0, rows[at])
            for step in range(8):
                value = value - factors[step] * pivots[step]
            rows[at] = value
        unit = jnp.where(lane < sub + first, top, 0.0) + jnp.where(lane == sub + first, 1.0, 0.0)
        result.append(unit * lax.rsqrt(pivot_col))
        if more:
            diagonal = coming
        yield


def stacked(value):
    high, low = split2(value)
    return jnp.concatenate(
        [jnp.concatenate([high, high], axis=1), jnp.concatenate([low, low], axis=1)], axis=0
    )


def panel_kernel(
    rounds_ref, aux_ref, table_ref, near_ref, far_ref, more_hbm, feat_hbm, prev_hbm,
    new_hbm, resid_ref, part_ref,
    more_ref, feat_ref, prev_ref, cols_ref, squares_ref,
    more_sem, in_sems, out_sems, *, tile, chunk,
):
    feat, points = feat_ref.shape
    width = prev_ref.shape[1]
    size = aux_ref.shape[1]
    chunks = points // chunk

    def incoming(at):
        here = pl.ds(at * chunk, chunk)
        return (
            pltpu.make_async_copy(feat_hbm.at[:, here], feat_ref.at[:, here], in_sems.at[0, at]),
            pltpu.make_async_copy(prev_hbm.at[here, :], prev_ref.at[here, :], in_sems.at[1, at]),
        )

    def outgoing(at):
        here = pl.ds(at * chunk, chunk)
        return pltpu.make_async_copy(cols_ref.at[here, :], new_hbm.at[here, :], out_sems.at[at])

    for at in range(chunks):
        for copy in incoming(at):
            copy.start()

    @pl.when(rounds_ref[0] > 1)
    def _():
        copy = pltpu.make_async_copy(more_hbm, more_ref, more_sem)
        copy.start()
        copy.wait()

    @pl.when(rounds_ref[0] <= 1)
    def _():
        more_ref[...] = jnp.zeros_like(more_ref)

    mine = aux_ref[0:1, :]
    scales_row = aux_ref[1:2, :feat]
    noise = aux_ref[2:3, :]
    scales_col = jnp.broadcast_to(aux_ref[1:2, :], (8, size)).T[:feat, :1]
    core = lax.rem(lax.axis_index("rows"), 2)
    rows = unpack(table_ref[...], near_ref[...], far_ref[...], core) + more_ref[...]
    piv_x = rows[:, :feat]
    piv_f = rows[:, 128:]
    piv_s = piv_x * scales_row
    piv_sq = jnp.sum(piv_s * piv_x, axis=1, keepdims=True)
    pad = jnp.zeros((size, 128 - feat), F32)
    lane = lax.broadcasted_iota(jnp.int32, (size, 128), 1)
    piv_left = jnp.concatenate([piv_x, pad], axis=1)
    piv_left = jnp.where(lane == feat, piv_sq, jnp.where(lane == feat + 1, 1.0, piv_left))
    piv_right = jnp.concatenate([piv_s, pad], axis=1)
    piv_right = jnp.where(lane == feat, -0.5, jnp.where(lane == feat + 1, -0.5 * piv_sq, piv_right))

    fac_rhs = stacked(piv_f)
    x_high, x_mid, x_low = split3(piv_right)
    x_rhs = jnp.concatenate(
        [jnp.concatenate([x_high, x_high], axis=1), jnp.concatenate([x_mid, x_mid], axis=1)], axis=0
    )
    x_rest = jnp.concatenate([x_low, x_high], axis=1)

    def kernel_of(left):
        high, mid, low_part = split3(left)
        two = lax.dot_general(jnp.concatenate([high, mid], axis=1), x_rhs, NT, preferred_element_type=F32)
        rest = lax.dot_general(jnp.concatenate([high, low_part], axis=1), x_rest, NT, preferred_element_type=F32)
        return jnp.exp(two[:, :size] + (two[:, size:] + rest))

    def earlier_of(fac):
        both = lax.dot_general(
            jnp.concatenate(split2(fac), axis=1), fac_rhs, NT, preferred_element_type=F32
        )
        return both[:, :size] + both[:, size:]

    row_id = lax.broadcasted_iota(jnp.int32, (size, size), 0)
    col_id = lax.broadcasted_iota(jnp.int32, (size, size), 1)
    block = kernel_of(piv_left) + jnp.where(row_id == col_id, noise, 0.0) - earlier_of(piv_f)
    inverse_rows = []
    steps = factor_steps(block, inverse_rows)

    sub = lax.broadcasted_iota(jnp.int32, (8, tile), 0)
    ids = lax.broadcasted_iota(jnp.int32, (tile, size), 0).astype(F32)

    def columns(base):
        here = pl.ds(base, tile)
        xt = feat_ref[:, here]
        length = jnp.sum(xt * xt * scales_col, axis=0, keepdims=True)
        extra = jnp.where(sub == 0, length, jnp.where(sub == 1, 1.0, 0.0))
        left = jnp.concatenate([xt, extra, jnp.zeros((128 - feat - 8, tile), F32)], axis=0).T
        kern = kernel_of(left) + jnp.where(ids == mine - base, noise, 0.0)
        fac = prev_ref[here, :]
        cols_ref[here, :] = kern - earlier_of(fac)
        total = fac[:, :128] * fac[:, :128]
        for start in range(128, width, 128):
            total = total + fac[:, start : start + 128] * fac[:, start : start + 128]
        squares_ref[here, :] = total

    for _ in range(3):
        next(steps, None)
    done = 0
    for at in range(points // tile):
        if at in (0, 6):
            for part in range({0: 3, 6: 5}[at]):
                for copy in incoming(done):
                    copy.wait()
                done += 1
        columns(at * tile)
        next(steps, None)
    for _ in steps:
        pass

    inv_rhs = stacked(jnp.concatenate(inverse_rows, axis=0))
    total = jnp.zeros((1, 128), F32)
    for at in range(chunks):
        for inner in range(chunk // tile):
            base = at * chunk + inner * tile
            here = pl.ds(base, tile)
            high, low_part = split2(cols_ref[here, :])
            both = lax.dot_general(
                jnp.concatenate([high, low_part], axis=1), inv_rhs, NT, preferred_element_type=F32
            )
            new = both[:, :size] + both[:, size:]
            cols_ref[here, :] = new
            gone = squares_ref[here, :] + new * new
            for sub_at in range(tile // 128):
                flipped = gone[sub_at * 128 : (sub_at + 1) * 128, :].T
                row = 1.0 + noise - jnp.sum(flipped, axis=0, keepdims=True)
                resid_ref[pl.ds(base // 128 + sub_at, 1), :] = row
                total = total + row
        outgoing(at).start()
    part_ref[...] = jnp.broadcast_to(jnp.sum(total, axis=1, keepdims=True), part_ref.shape)
    for at in range(chunks):
        outgoing(at).wait()


def run_panel(devices, rounds, aux, table, near, far, more, feat_t, prev):
    feat, points = feat_t.shape
    width = prev.shape[1]
    size = aux.shape[1]
    chunk = 512
    return pl.pallas_call(
        functools.partial(panel_kernel, tile=256, chunk=chunk),
        out_shape=(
            jax.ShapeDtypeStruct((points, size), F32),
            jax.ShapeDtypeStruct((points // 128, 128), F32),
            jax.ShapeDtypeStruct((devices, 128), F32),
        ),
        in_specs=[SMEM] + [VMEM] * 4 + [ANY] * 3,
        out_specs=(ANY, VMEM, VMEM),
        scratch_shapes=[
            pltpu.VMEM(more.shape, F32),
            pltpu.VMEM((feat, points), F32),
            pltpu.VMEM((points, width), F32),
            pltpu.VMEM((points, size), F32),
            pltpu.VMEM((points, 128), F32),
            pltpu.SemaphoreType.DMA,
            pltpu.SemaphoreType.DMA((2, points // chunk)),
            pltpu.SemaphoreType.DMA((points // chunk,)),
        ],
        compiler_params=pltpu.CompilerParams(vmem_limit_bytes=PANEL),
        name="panel",
    )(rounds, aux, table, near, far, more, feat_t, prev)


def local(devices, features, prev_factors, inv_scales, noise, pivot_owner, pivot_local):
    points, feat = features.shape
    feat_t = features.T
    layer = groups_of(devices, ((1, 2), (16, 16)))
    column = groups_of(devices, ((2, LAYERS),))
    cores = [(at, at ^ 1) for at in range(devices)]

    def fetch(at_round):
        picked = run_pick(at_round, pivot_owner, pivot_local, feat_t, prev_factors)
        landed = exchange(picked.reshape(32, RANKS, 256), layer)
        pack_table, table, aux, more, rounds = run_table(
            at_round, noise, pivot_owner, pivot_local, inv_scales.reshape(1, feat)
        )
        packed = run_pack(pack_table, landed.reshape(32 * RANKS, 256))
        near = exchange(packed, column)
        return table, near, lax.ppermute(near, "rows", cores), aux, more, rounds

    def again(carry):
        at_round, more = carry
        table, near, far, *_ = fetch(at_round.reshape(1))
        return at_round + 1, more + unpack(table, near, far, lax.rem(lax.axis_index("rows"), 2))

    table, near, far, aux, more, rounds = fetch(jnp.zeros((1,), jnp.int32))
    _, more = lax.while_loop(lambda carry: carry[0] < rounds[0], again, (jnp.int32(1), more))
    new_factors, resid, part = run_panel(devices, rounds, aux, table, near, far, more, feat_t, prev_factors)
    sums = exchange(part.reshape(devices, 1, 128), None)
    trace = jnp.sum(sums[:, 0, 0]).reshape(1)
    return new_factors, resid.reshape(points), trace


def solution(mesh):
    placed = (P("rows", None), P("rows", None), P(), P(), P(), P())
    return jax.shard_map(
        functools.partial(local, mesh.shape["rows"]),
        mesh=mesh,
        in_specs=placed,
        out_specs=(P("rows", None), P("rows"), P()),
        check_vma=False,
    )
```

```python
import functools

import jax
import jax.numpy as jnp
from jax import lax
from jax.experimental import pallas as pl
from jax.experimental.pallas import tpu as pltpu
from jax.sharding import PartitionSpec as P

F32 = jnp.float32
BF16 = jnp.bfloat16
HIGH = lax.Precision.HIGHEST
VMEM = pl.BlockSpec(memory_space=pltpu.VMEM)
SMEM = pl.BlockSpec(memory_space=pltpu.SMEM)
ANY = pl.BlockSpec(memory_space=pl.ANY)
HBM = pl.BlockSpec(memory_space=pltpu.HBM)
NT = (((1,), (1,)), ((), ()))
SMALL = 16 * 1024 * 1024
PANEL = 60000000
LAYERS = 8
RANKS = 8
SPOTS = 32
SPLITS = 4


def groups_of(total, fields):
    found = {}
    for index in range(total):
        key = index
        for stride, size in fields:
            key -= ((index // stride) % size) * stride
        found.setdefault(key, []).append(index)
    return list(found.values())


def exchange(blocks, groups):
    return lax.all_to_all(blocks, "rows", 0, 0, axis_index_groups=groups, tiled=True)


def pick_kernel(
    round_ref, owner_hbm, place_hbm, feat_hbm, prev_hbm, out_ref, owner_ref, place_ref, feat_part, prev_part,
    found, table_sems, sems,
):
    tables = (
        pltpu.make_async_copy(owner_hbm, owner_ref, table_sems.at[0]),
        pltpu.make_async_copy(place_hbm, place_ref, table_sems.at[1]),
    )
    for copy in tables:
        copy.start()
    feat_part[...] = jnp.zeros_like(feat_part)
    panels, panel = owner_ref.shape
    feat = feat_hbm.shape[0]
    me = lax.axis_index("rows")
    first = (round_ref[0] // SPLITS) * RANKS
    for copy in tables:
        copy.wait()
    count = jnp.int32(0)
    for pivot in range(panels * panel):
        found[count] = pivot
        count = count + (owner_ref[pivot // panel, pivot % panel] == me).astype(jnp.int32)
    count = jnp.clip(count - first, 0, RANKS)

    def place_of(at):
        pivot = found[first + at]
        return place_ref[pivot // panel, lax.rem(pivot, panel)]

    def copies(at):
        place = place_of(at)
        wide = pl.ds(pl.multiple_of((place // 128) * 128, 128), 128)
        rows = pl.ds(pl.multiple_of((place // 8) * 8, 8), 8)
        return (
            pltpu.make_async_copy(feat_hbm.at[:, wide], feat_part.at[at], sems.at[0, at]),
            pltpu.make_async_copy(prev_hbm.at[rows, :], prev_part.at[at], sems.at[1, at]),
        )

    def start(at, carry):
        for copy in copies(at):
            copy.start()
        return carry

    def land(at, carry):
        for copy in copies(at):
            copy.wait()
        return carry

    lax.fori_loop(0, count, start, 0)
    lax.fori_loop(0, count, land, 0)

    @pl.when(count > 0)
    def _():
        lane = lax.broadcasted_iota(jnp.int32, (feat, 128), 1)
        fac_sub = lax.broadcasted_iota(jnp.int32, prev_part.shape[1:], 0)
        xs, facs = jnp.zeros((feat, 128), F32), []
        for at in range(RANKS):
            used = at < count
            place = place_of(jnp.where(used, at, 0))
            x = jnp.where((lane == lax.rem(place, 128)) & used, feat_part[at], 0.0)
            xs = jnp.where(lane == at, jnp.sum(x, axis=1, keepdims=True), xs)
            fac = jnp.where((fac_sub == lax.rem(place, 8)) & used, prev_part[at], 0.0)
            facs.append(jnp.sum(fac, axis=0, keepdims=True))
        xs = jnp.concatenate([xs, jnp.zeros((128 - feat, 128), F32)], axis=0).T[:RANKS]
        facs = jnp.concatenate(facs, axis=0)
        halves = (jnp.concatenate([xs, facs[:, :128]], axis=1), facs[:, 128:])
        for at in range(out_ref.shape[0]):
            for half in range(2):
                out_ref[at, half] = halves[half]

    @pl.when(count == 0)
    def _():
        out_ref[...] = jnp.zeros_like(out_ref)


def run_pick(at_round, pivot_owner, pivot_local, feat_t, prev):
    return pl.pallas_call(
        pick_kernel,
        out_shape=jax.ShapeDtypeStruct((16, 2, RANKS, 256), F32),
        in_specs=[SMEM, HBM, HBM, HBM, HBM],
        out_specs=VMEM,
        scratch_shapes=[
            pltpu.SMEM(pivot_owner.shape, jnp.int32),
            pltpu.SMEM(pivot_local.shape, jnp.int32),
            pltpu.VMEM((RANKS, feat_t.shape[0], 128), F32),
            pltpu.VMEM((RANKS, 8, prev.shape[1]), F32),
            pltpu.SMEM((pivot_owner.size + 1,), jnp.int32),
            pltpu.SemaphoreType.DMA((2,)),
            pltpu.SemaphoreType.DMA((2, RANKS)),
        ],
        compiler_params=pltpu.CompilerParams(vmem_limit_bytes=64 * 1024 * 1024),
        name="pick",
    )(at_round, pivot_owner, pivot_local, feat_t, prev)


def table_kernel(
    round_ref, noise_ref, owner_ref, place_ref, scales_ref, pack_ref, pivots_ref, aux_ref, more_ref, rounds_ref
):
    panels, panel = owner_ref.shape
    size = panels * panel
    at_round = round_ref[0]
    window_now = (at_round // SPLITS).astype(F32)
    split_now = lax.rem(at_round, SPLITS).astype(F32)
    layer_now = lax.rem(lax.axis_index("rows") // 2, LAYERS).astype(F32)
    owner_row = jnp.concatenate([owner_ref[at : at + 1, :] for at in range(panels)], axis=1).astype(F32)
    place_row = jnp.concatenate([place_ref[at : at + 1, :] for at in range(panels)], axis=1).astype(F32)
    mine = jnp.where(owner_row == lax.axis_index("rows").astype(F32), place_row, -1.0)
    scales = jnp.concatenate([scales_ref[...], jnp.zeros_like(scales_ref)], axis=1)
    sub = lax.broadcasted_iota(jnp.int32, aux_ref.shape, 0)
    aux_ref[...] = jnp.where(sub == 0, mine, jnp.where(sub == 1, scales, noise_ref[0]))
    more_ref[...] = jnp.zeros_like(more_ref)
    owner_row = jnp.broadcast_to(owner_row, (size, size))
    owner_col = owner_row.T
    row_id = lax.broadcasted_iota(jnp.int32, (size, size), 0)
    col_id = lax.broadcasted_iota(jnp.int32, (size, size), 1)
    earlier = col_id < row_id

    def whole(value, unit):
        return jnp.floor(value * (1.0 / unit))

    def rest(value, unit):
        return value - unit * whole(value, unit)

    def ranks(same):
        found = jnp.sum(jnp.where(same & earlier, 1.0, 0.0), axis=1, keepdims=True)
        return jnp.broadcast_to(found, (size, size))

    rank = ranks(owner_row == owner_col)
    window = whole(rank, RANKS)
    layer_row = rest(whole(owner_row, 2), LAYERS)
    layer_col = rest(whole(owner_col, 2), LAYERS)
    spot = ranks((layer_row == layer_col) & (window == window.T))
    split = whole(spot, SPOTS)
    spot = rest(spot, SPOTS)
    active = (window == window_now) & (split == split_now)
    rounds_ref[0] = jnp.max(window * SPLITS + split).astype(jnp.int32) + 1

    wide = lax.broadcasted_iota(jnp.int32, (size, LAYERS * SPOTS), 1).astype(F32)
    both = lambda value: jnp.concatenate([value, value], axis=1)
    goal = both(jnp.where(active, layer_col * SPOTS + spot, -1.0))
    pivots_ref[...] = jnp.where(wide == goal, 1.0, 0.0)
    origin = (whole(owner_col, 2 * LAYERS) * 2 + rest(owner_col, 2)) * RANKS + rest(rank, RANKS)
    origin = jnp.where(wide == both(origin), 1.0, 0.0).astype(BF16)
    spot_row = jnp.where(active & (layer_col == layer_now), spot, -1.0).T[:SPOTS]
    target = lax.broadcasted_iota(jnp.int32, (SPOTS, size), 0).astype(F32)
    target = jnp.where(spot_row == target, 1.0, 0.0).astype(BF16)
    pack_ref[...] = jnp.dot(target, origin, preferred_element_type=F32)


def run_table(at_round, noise, pivot_owner, pivot_local, scales):
    size = pivot_owner.size
    return pl.pallas_call(
        table_kernel,
        out_shape=(
            jax.ShapeDtypeStruct((SPOTS, 32 * RANKS), F32),
            jax.ShapeDtypeStruct((size, LAYERS * SPOTS), F32),
            jax.ShapeDtypeStruct((8, size), F32),
            jax.ShapeDtypeStruct((size, 512), F32),
            jax.ShapeDtypeStruct((1,), jnp.int32),
        ),
        in_specs=[SMEM, SMEM, VMEM, VMEM, VMEM],
        out_specs=(VMEM, VMEM, VMEM, VMEM, SMEM),
        compiler_params=pltpu.CompilerParams(vmem_limit_bytes=SMALL),
        name="table",
    )(at_round, noise, pivot_owner, pivot_local, scales)


def pack_kernel(table_ref, rows_ref, out_ref):
    packed = pick_rows(table_ref[...], rows_ref[...])
    for at in range(out_ref.shape[0]):
        out_ref[at] = packed


def run_pack(table, rows):
    return pl.pallas_call(
        pack_kernel,
        out_shape=jax.ShapeDtypeStruct((LAYERS, SPOTS, 256), F32),
        in_specs=[VMEM, VMEM],
        out_specs=VMEM,
        compiler_params=pltpu.CompilerParams(vmem_limit_bytes=SMALL),
        name="pack",
    )(table, rows)


def unpack(table, near, far, core):
    first = jnp.where(core == 0, near, far).reshape(LAYERS * SPOTS, 256)
    second = jnp.where(core == 0, far, near).reshape(LAYERS * SPOTS, 256)
    return pick_rows(table, jnp.concatenate([first, second], axis=1))


def pick_rows(table, rows):
    table = table.astype(BF16)
    high, mid, low = [jnp.dot(table, part, preferred_element_type=F32) for part in split3(rows)]
    return high + mid + low


def split2(value):
    high = value.astype(BF16)
    return high, (value - high.astype(F32)).astype(BF16)


def split3(value):
    high = value.astype(BF16)
    rest = value - high.astype(F32)
    mid = rest.astype(BF16)
    return high, mid, (rest - mid.astype(F32)).astype(BF16)


def factor_steps(block, result):
    size = block.shape[0]
    count = size // 8
    rows = [block[8 * at : 8 * at + 8] for at in range(count)]
    lane = lax.broadcasted_iota(jnp.int32, (8, size), 1)
    sub = lax.broadcasted_iota(jnp.int32, (8, size), 0)

    def spread_row(value, row):
        return jnp.broadcast_to(value[row : row + 1], (8, size))

    def spread_columns(value, first):
        return [jnp.broadcast_to(value[:, first + k : first + k + 1], (8, size)) for k in range(8)]

    diagonal = spread_columns(rows[0], 0)
    for home in range(count):
        first = 8 * home
        more = home + 1 < count
        inside = (lane >= first) & (lane < first + 8)
        top = jnp.where(inside, 0.0, rows[home])
        pivots, inverses, ahead, pivot_col = [], [], {}, None
        if more:
            below = spread_columns(rows[home + 1], first)
            coming = spread_columns(rows[home + 1], first + 8)
            below_factors = []
        for step in range(8):
            pivot = spread_row(diagonal[step], step)
            pivot_col = pivot if pivot_col is None else jnp.where(sub == step, pivot, pivot_col)
            inverse = 1.0 / pivot
            inverses.append(inverse)
            factor = jnp.where(sub > step, diagonal[step] * inverse, 0.0)
            for k in range(step + 1, 8):
                ahead[k, step] = spread_row(diagonal[k], step)
                diagonal[k] = diagonal[k] - factor * ahead[k, step]
            if more:
                part = below[step] * inverse
                below_factors.append(part)
                for k in range(step + 1, 8):
                    below[k] = below[k] - part * ahead[k, step]
                for k in range(8):
                    coming[k] = coming[k] - part * spread_row(below[step], k)
            row = jnp.where(lane == first + step, 1.0, spread_row(top, step))
            pivots.append(row)
            if step < 7:
                top = top - factor * row
        for at in range(home + 1, count):
            if at == home + 1:
                factors = below_factors
            else:
                columns = spread_columns(rows[at], first)
                factors = []
                for step in range(8):
                    part = columns[step] * inverses[step]
                    factors.append(part)
                    for k in range(step + 1, 8):
                        columns[k] = columns[k] - part * ahead[k, step]
            value = jnp.where(inside, 0.0, rows[at])
            for step in range(8):
                value = value - factors[step] * pivots[step]
            rows[at] = value
        unit = jnp.where(lane < sub + first, top, 0.0) + jnp.where(lane == sub + first, 1.0, 0.0)
        result.append(unit * lax.rsqrt(pivot_col))
        if more:
            diagonal = coming
        yield


def halved_steps(block, result):
    half = block.shape[0] // 2
    upper, lower = [], []
    yield from factor_steps(block[:half, :half], upper)
    upper = jnp.concatenate(upper, axis=0)
    joint = lax.dot_general(block[half:, :half], upper, NT, precision=HIGH, preferred_element_type=F32)
    rest = lax.dot_general(joint, joint, NT, precision=HIGH, preferred_element_type=F32)
    joint = jnp.dot(joint, upper, precision=HIGH, preferred_element_type=F32)
    yield from factor_steps(block[half:, half:] - rest, lower)
    lower = jnp.concatenate(lower, axis=0)
    joint = jnp.dot(lower, joint, precision=HIGH, preferred_element_type=F32)
    result.append(jnp.concatenate([upper, jnp.zeros_like(upper)], axis=1))
    result.append(jnp.concatenate([-joint, lower], axis=1))


def stacked(value):
    high, low = split2(value)
    return jnp.concatenate(
        [jnp.concatenate([high, high], axis=1), jnp.concatenate([low, low], axis=1)], axis=0
    )


def panel_kernel(
    rounds_ref, aux_ref, table_ref, near_ref, far_ref, more_hbm, feat_hbm, prev_hbm,
    new_hbm, resid_ref, part_ref,
    more_ref, feat_ref, prev_ref, cols_ref, squares_ref,
    more_sem, in_sems, out_sems, *, tile, chunk,
):
    feat, points = feat_ref.shape
    width = prev_ref.shape[1]
    size = aux_ref.shape[1]
    chunks = points // chunk

    def incoming(at):
        here = pl.ds(at * chunk, chunk)
        return (
            pltpu.make_async_copy(feat_hbm.at[:, here], feat_ref.at[:, here], in_sems.at[0, at]),
            pltpu.make_async_copy(prev_hbm.at[here, :], prev_ref.at[here, :], in_sems.at[1, at]),
        )

    def outgoing(at):
        here = pl.ds(at * chunk, chunk)
        return pltpu.make_async_copy(cols_ref.at[here, :], new_hbm.at[here, :], out_sems.at[at])

    for at in range(chunks):
        for copy in incoming(at):
            copy.start()

    @pl.when(rounds_ref[0] > 1)
    def _():
        copy = pltpu.make_async_copy(more_hbm, more_ref, more_sem)
        copy.start()
        copy.wait()

    @pl.when(rounds_ref[0] <= 1)
    def _():
        more_ref[...] = jnp.zeros_like(more_ref)

    mine = aux_ref[0:1, :]
    scales_row = aux_ref[1:2, :feat]
    noise = aux_ref[2:3, :]
    scales_col = jnp.broadcast_to(aux_ref[1:2, :], (8, size)).T[:feat, :1]
    core = lax.rem(lax.axis_index("rows"), 2)
    rows = unpack(table_ref[...], near_ref[...], far_ref[...], core) + more_ref[...]
    piv_x = rows[:, :feat]
    piv_f = rows[:, 128:]
    piv_s = piv_x * scales_row
    piv_sq = jnp.sum(piv_s * piv_x, axis=1, keepdims=True)
    pad = jnp.zeros((size, 128 - feat), F32)
    lane = lax.broadcasted_iota(jnp.int32, (size, 128), 1)
    piv_left = jnp.concatenate([piv_x, pad], axis=1)
    piv_left = jnp.where(lane == feat, piv_sq, jnp.where(lane == feat + 1, 1.0, piv_left))
    piv_right = jnp.concatenate([piv_s, pad], axis=1)
    piv_right = jnp.where(lane == feat, -0.5, jnp.where(lane == feat + 1, -0.5 * piv_sq, piv_right))

    fac_rhs = stacked(piv_f)
    x_high, x_mid, x_low = split3(piv_right)
    x_rhs = jnp.concatenate(
        [jnp.concatenate([x_high, x_high], axis=1), jnp.concatenate([x_mid, x_mid], axis=1)], axis=0
    )
    x_rest = jnp.concatenate([x_low, x_high], axis=1)

    def kernel_of(left):
        high, mid, low_part = split3(left)
        two = lax.dot_general(jnp.concatenate([high, mid], axis=1), x_rhs, NT, preferred_element_type=F32)
        rest = lax.dot_general(jnp.concatenate([high, low_part], axis=1), x_rest, NT, preferred_element_type=F32)
        return jnp.exp(two[:, :size] + (two[:, size:] + rest))

    def earlier_of(fac):
        both = lax.dot_general(
            jnp.concatenate(split2(fac), axis=1), fac_rhs, NT, preferred_element_type=F32
        )
        return both[:, :size] + both[:, size:]

    row_id = lax.broadcasted_iota(jnp.int32, (size, size), 0)
    col_id = lax.broadcasted_iota(jnp.int32, (size, size), 1)
    block = kernel_of(piv_left) + jnp.where(row_id == col_id, noise, 0.0) - earlier_of(piv_f)
    inverse_rows = []
    steps = halved_steps(block, inverse_rows)

    sub = lax.broadcasted_iota(jnp.int32, (8, tile), 0)
    ids = lax.broadcasted_iota(jnp.int32, (tile, size), 0).astype(F32)

    def columns(base):
        here = pl.ds(base, tile)
        xt = feat_ref[:, here]
        length = jnp.sum(xt * xt * scales_col, axis=0, keepdims=True)
        extra = jnp.where(sub == 0, length, jnp.where(sub == 1, 1.0, 0.0))
        left = jnp.concatenate([xt, extra, jnp.zeros((128 - feat - 8, tile), F32)], axis=0).T
        kern = kernel_of(left) + jnp.where(ids == mine - base, noise, 0.0)
        fac = prev_ref[here, :]
        cols_ref[here, :] = kern - earlier_of(fac)
        total = fac[:, :128] * fac[:, :128]
        for start in range(128, width, 128):
            total = total + fac[:, start : start + 128] * fac[:, start : start + 128]
        squares_ref[here, :] = total

    for _ in range(5):
        next(steps, None)
    done = 0
    for at in range(points // tile):
        if at in (0, 6):
            for part in range({0: 3, 6: 5}[at]):
                for copy in incoming(done):
                    copy.wait()
                done += 1
        columns(at * tile)
        next(steps, None)
    for _ in steps:
        pass

    inv_rhs = stacked(jnp.concatenate(inverse_rows, axis=0))
    total = jnp.zeros((1, 128), F32)
    for at in range(chunks):
        for inner in range(chunk // tile):
            base = at * chunk + inner * tile
            here = pl.ds(base, tile)
            high, low_part = split2(cols_ref[here, :])
            both = lax.dot_general(
                jnp.concatenate([high, low_part], axis=1), inv_rhs, NT, preferred_element_type=F32
            )
            new = both[:, :size] + both[:, size:]
            cols_ref[here, :] = new
            gone = squares_ref[here, :] + new * new
            for sub_at in range(tile // 128):
                flipped = gone[sub_at * 128 : (sub_at + 1) * 128, :].T
                row = 1.0 + noise - jnp.sum(flipped, axis=0, keepdims=True)
                resid_ref[pl.ds(base // 128 + sub_at, 1), :] = row
                total = total + row
        outgoing(at).start()
    part_ref[...] = jnp.broadcast_to(jnp.sum(total, axis=1, keepdims=True), part_ref.shape)
    for at in range(chunks):
        outgoing(at).wait()


def run_panel(devices, rounds, aux, table, near, far, more, feat_t, prev):
    feat, points = feat_t.shape
    width = prev.shape[1]
    size = aux.shape[1]
    chunk = 512
    return pl.pallas_call(
        functools.partial(panel_kernel, tile=256, chunk=chunk),
        out_shape=(
            jax.ShapeDtypeStruct((points, size), F32),
            jax.ShapeDtypeStruct((points // 128, 128), F32),
            jax.ShapeDtypeStruct((devices, 128), F32),
        ),
        in_specs=[SMEM] + [VMEM] * 4 + [ANY] * 3,
        out_specs=(ANY, VMEM, VMEM),
        scratch_shapes=[
            pltpu.VMEM(more.shape, F32),
            pltpu.VMEM((feat, points), F32),
            pltpu.VMEM((points, width), F32),
            pltpu.VMEM((points, size), F32),
            pltpu.VMEM((points, 128), F32),
            pltpu.SemaphoreType.DMA,
            pltpu.SemaphoreType.DMA((2, points // chunk)),
            pltpu.SemaphoreType.DMA((points // chunk,)),
        ],
        compiler_params=pltpu.CompilerParams(vmem_limit_bytes=PANEL),
        name="panel",
    )(rounds, aux, table, near, far, more, feat_t, prev)


def local(devices, features, prev_factors, inv_scales, noise, pivot_owner, pivot_local):
    points, feat = features.shape
    feat_t = features.T
    layer = groups_of(devices, ((1, 2), (16, 16)))
    column = groups_of(devices, ((2, LAYERS),))
    cores = [(at, at ^ 1) for at in range(devices)]

    def fetch(at_round):
        picked = run_pick(at_round, pivot_owner, pivot_local, feat_t, prev_factors)
        landed = exchange(picked.reshape(32, RANKS, 256), layer)
        pack_table, table, aux, more, rounds = run_table(
            at_round, noise, pivot_owner, pivot_local, inv_scales.reshape(1, feat)
        )
        packed = run_pack(pack_table, landed.reshape(32 * RANKS, 256))
        near = exchange(packed, column)
        return table, near, lax.ppermute(near, "rows", cores), aux, more, rounds

    def again(carry):
        at_round, more = carry
        table, near, far, *_ = fetch(at_round.reshape(1))
        return at_round + 1, more + unpack(table, near, far, lax.rem(lax.axis_index("rows"), 2))

    table, near, far, aux, more, rounds = fetch(jnp.zeros((1,), jnp.int32))
    _, more = lax.while_loop(lambda carry: carry[0] < rounds[0], again, (jnp.int32(1), more))
    new_factors, resid, part = run_panel(devices, rounds, aux, table, near, far, more, feat_t, prev_factors)
    sums = exchange(part.reshape(devices, 1, 128), None)
    trace = jnp.sum(sums[:, 0, 0]).reshape(1)
    return new_factors, resid.reshape(points), trace


def solution(mesh):
    placed = (P("rows", None), P("rows", None), P(), P(), P(), P())
    return jax.shard_map(
        functools.partial(local, mesh.shape["rows"]),
        mesh=mesh,
        in_specs=placed,
        out_specs=(P("rows", None), P("rows"), P()),
        check_vma=False,
    )
```

```python
import functools

import jax
import jax.numpy as jnp
from jax import lax
from jax.experimental import pallas as pl
from jax.experimental.pallas import tpu as pltpu
from jax.sharding import PartitionSpec as P

F32 = jnp.float32
BF16 = jnp.bfloat16
HIGH = lax.Precision.HIGHEST
VMEM = pl.BlockSpec(memory_space=pltpu.VMEM)
SMEM = pl.BlockSpec(memory_space=pltpu.SMEM)
ANY = pl.BlockSpec(memory_space=pl.ANY)
HBM = pl.BlockSpec(memory_space=pltpu.HBM)
NT = (((1,), (1,)), ((), ()))
SMALL = 16 * 1024 * 1024
PANEL = 60000000
ROUNDS = 64
LAYERS = 8
RANKS = 8
SPOTS = 32
SPLITS = 4


def groups_of(total, fields):
    found = {}
    for index in range(total):
        key = index
        for stride, size in fields:
            key -= ((index // stride) % size) * stride
        found.setdefault(key, []).append(index)
    return list(found.values())


def exchange(blocks, groups):
    return lax.all_to_all(blocks, "rows", 0, 0, axis_index_groups=groups, tiled=True)


def pick_kernel(
    round_ref, owner_hbm, place_hbm, feat_hbm, prev_hbm, out_ref, owner_ref, place_ref, feat_part, prev_part,
    found, table_sems, sems,
):
    tables = (
        pltpu.make_async_copy(owner_hbm, owner_ref, table_sems.at[0]),
        pltpu.make_async_copy(place_hbm, place_ref, table_sems.at[1]),
    )
    for copy in tables:
        copy.start()
    feat_part[...] = jnp.zeros_like(feat_part)
    panels, panel = owner_ref.shape
    feat = feat_hbm.shape[0]
    me = lax.axis_index("rows")
    first = (round_ref[0] // SPLITS) * RANKS
    for copy in tables:
        copy.wait()
    count = jnp.int32(0)
    for pivot in range(panels * panel):
        found[count] = pivot
        count = count + (owner_ref[pivot // panel, pivot % panel] == me).astype(jnp.int32)
    count = jnp.clip(count - first, 0, RANKS)

    def place_of(at):
        pivot = found[first + at]
        return place_ref[pivot // panel, lax.rem(pivot, panel)]

    def copies(at):
        place = place_of(at)
        wide = pl.ds(pl.multiple_of((place // 128) * 128, 128), 128)
        rows = pl.ds(pl.multiple_of((place // 8) * 8, 8), 8)
        return (
            pltpu.make_async_copy(feat_hbm.at[:, wide], feat_part.at[at], sems.at[0, at]),
            pltpu.make_async_copy(prev_hbm.at[rows, :], prev_part.at[at], sems.at[1, at]),
        )

    def start(at, carry):
        for copy in copies(at):
            copy.start()
        return carry

    def land(at, carry):
        for copy in copies(at):
            copy.wait()
        return carry

    lax.fori_loop(0, count, start, 0)
    lax.fori_loop(0, count, land, 0)

    @pl.when(count > 0)
    def _():
        lane = lax.broadcasted_iota(jnp.int32, (feat, 128), 1)
        fac_sub = lax.broadcasted_iota(jnp.int32, prev_part.shape[1:], 0)
        xs, facs = jnp.zeros((feat, 128), F32), []
        for at in range(RANKS):
            used = at < count
            place = place_of(jnp.where(used, at, 0))
            x = jnp.where((lane == lax.rem(place, 128)) & used, feat_part[at], 0.0)
            xs = jnp.where(lane == at, jnp.sum(x, axis=1, keepdims=True), xs)
            fac = jnp.where((fac_sub == lax.rem(place, 8)) & used, prev_part[at], 0.0)
            facs.append(jnp.sum(fac, axis=0, keepdims=True))
        xs = jnp.concatenate([xs, jnp.zeros((128 - feat, 128), F32)], axis=0).T[:RANKS]
        facs = jnp.concatenate(facs, axis=0)
        halves = (jnp.concatenate([xs, facs[:, :128]], axis=1), facs[:, 128:])
        for at in range(out_ref.shape[0]):
            for half in range(2):
                out_ref[at, half] = halves[half]

    @pl.when(count == 0)
    def _():
        out_ref[...] = jnp.zeros_like(out_ref)


def run_pick(at_round, pivot_owner, pivot_local, feat_t, prev):
    return pl.pallas_call(
        pick_kernel,
        out_shape=jax.ShapeDtypeStruct((16, 2, RANKS, 256), F32),
        in_specs=[SMEM, HBM, HBM, HBM, HBM],
        out_specs=VMEM,
        scratch_shapes=[
            pltpu.SMEM(pivot_owner.shape, jnp.int32),
            pltpu.SMEM(pivot_local.shape, jnp.int32),
            pltpu.VMEM((RANKS, feat_t.shape[0], 128), F32),
            pltpu.VMEM((RANKS, 8, prev.shape[1]), F32),
            pltpu.SMEM((pivot_owner.size + 1,), jnp.int32),
            pltpu.SemaphoreType.DMA((2,)),
            pltpu.SemaphoreType.DMA((2, RANKS)),
        ],
        compiler_params=pltpu.CompilerParams(vmem_limit_bytes=64 * 1024 * 1024),
        name="pick",
    )(at_round, pivot_owner, pivot_local, feat_t, prev)


def table_kernel(
    round_ref, noise_ref, owner_ref, place_ref, scales_ref, pack_ref, pivots_ref, aux_ref, more_ref, rounds_ref
):
    panels, panel = owner_ref.shape
    size = panels * panel
    at_round = round_ref[0]
    window_now = (at_round // SPLITS).astype(F32)
    split_now = lax.rem(at_round, SPLITS).astype(F32)
    layer_now = lax.rem(lax.axis_index("rows") // 2, LAYERS).astype(F32)
    owner_row = jnp.concatenate([owner_ref[at : at + 1, :] for at in range(panels)], axis=1).astype(F32)
    place_row = jnp.concatenate([place_ref[at : at + 1, :] for at in range(panels)], axis=1).astype(F32)
    mine = jnp.where(owner_row == lax.axis_index("rows").astype(F32), place_row, -1.0)
    scales = jnp.concatenate([scales_ref[...], jnp.zeros_like(scales_ref)], axis=1)
    sub = lax.broadcasted_iota(jnp.int32, aux_ref.shape, 0)
    aux_ref[...] = jnp.where(sub == 0, mine, jnp.where(sub == 1, scales, noise_ref[0]))
    more_ref[...] = jnp.zeros_like(more_ref)
    owner_row = jnp.broadcast_to(owner_row, (size, size))
    owner_col = owner_row.T
    row_id = lax.broadcasted_iota(jnp.int32, (size, size), 0)
    col_id = lax.broadcasted_iota(jnp.int32, (size, size), 1)
    earlier = col_id < row_id

    def whole(value, unit):
        return jnp.floor(value * (1.0 / unit))

    def rest(value, unit):
        return value - unit * whole(value, unit)

    def ranks(same):
        found = jnp.sum(jnp.where(same & earlier, 1.0, 0.0), axis=1, keepdims=True)
        return jnp.broadcast_to(found, (size, size))

    rank = ranks(owner_row == owner_col)
    window = whole(rank, RANKS)
    layer_row = rest(whole(owner_row, 2), LAYERS)
    layer_col = rest(whole(owner_col, 2), LAYERS)
    spot = ranks((layer_row == layer_col) & (window == window.T))
    split = whole(spot, SPOTS)
    spot = rest(spot, SPOTS)
    active = (window == window_now) & (split == split_now)
    number = window * SPLITS + split
    later = number > at_round.astype(F32)
    rounds_ref[0] = jnp.min(jnp.where(later, number, float(ROUNDS))).astype(jnp.int32)

    wide = lax.broadcasted_iota(jnp.int32, (size, LAYERS * SPOTS), 1).astype(F32)
    both = lambda value: jnp.concatenate([value, value], axis=1)
    goal = both(jnp.where(active, layer_col * SPOTS + spot, -1.0))
    pivots_ref[...] = jnp.where(wide == goal, 1.0, 0.0)
    origin = (whole(owner_col, 2 * LAYERS) * 2 + rest(owner_col, 2)) * RANKS + rest(rank, RANKS)
    origin = jnp.where(wide == both(origin), 1.0, 0.0).astype(BF16)
    spot_row = jnp.where(active & (layer_col == layer_now), spot, -1.0).T[:SPOTS]
    target = lax.broadcasted_iota(jnp.int32, (SPOTS, size), 0).astype(F32)
    target = jnp.where(spot_row == target, 1.0, 0.0).astype(BF16)
    pack_ref[...] = jnp.dot(target, origin, preferred_element_type=F32)


def run_table(at_round, noise, pivot_owner, pivot_local, scales):
    size = pivot_owner.size
    return pl.pallas_call(
        table_kernel,
        out_shape=(
            jax.ShapeDtypeStruct((SPOTS, 32 * RANKS), F32),
            jax.ShapeDtypeStruct((size, LAYERS * SPOTS), F32),
            jax.ShapeDtypeStruct((8, size), F32),
            jax.ShapeDtypeStruct((size, 512), F32),
            jax.ShapeDtypeStruct((1,), jnp.int32),
        ),
        in_specs=[SMEM, SMEM, VMEM, VMEM, VMEM],
        out_specs=(VMEM, VMEM, VMEM, VMEM, SMEM),
        compiler_params=pltpu.CompilerParams(vmem_limit_bytes=SMALL),
        name="table",
    )(at_round, noise, pivot_owner, pivot_local, scales)


def pack_kernel(table_ref, rows_ref, out_ref):
    packed = pick_rows(table_ref[...], rows_ref[...])
    for at in range(out_ref.shape[0]):
        out_ref[at] = packed


def run_pack(table, rows):
    return pl.pallas_call(
        pack_kernel,
        out_shape=jax.ShapeDtypeStruct((LAYERS, SPOTS, 256), F32),
        in_specs=[VMEM, VMEM],
        out_specs=VMEM,
        compiler_params=pltpu.CompilerParams(vmem_limit_bytes=SMALL),
        name="pack",
    )(table, rows)


def unpack(table, near, far, core):
    first = jnp.where(core == 0, near, far).reshape(LAYERS * SPOTS, 256)
    second = jnp.where(core == 0, far, near).reshape(LAYERS * SPOTS, 256)
    return pick_rows(table, jnp.concatenate([first, second], axis=1))


def pick_rows(table, rows):
    table = table.astype(BF16)
    high, mid, low = [jnp.dot(table, part, preferred_element_type=F32) for part in split3(rows)]
    return high + mid + low


def split2(value):
    high = value.astype(BF16)
    return high, (value - high.astype(F32)).astype(BF16)


def split3(value):
    high = value.astype(BF16)
    rest = value - high.astype(F32)
    mid = rest.astype(BF16)
    return high, mid, (rest - mid.astype(F32)).astype(BF16)


def factor_steps(block, result):
    size = block.shape[0]
    count = size // 8
    rows = [block[8 * at : 8 * at + 8] for at in range(count)]
    lane = lax.broadcasted_iota(jnp.int32, (8, size), 1)
    sub = lax.broadcasted_iota(jnp.int32, (8, size), 0)

    def spread_row(value, row):
        return jnp.broadcast_to(value[row : row + 1], (8, size))

    def spread_columns(value, first):
        return [jnp.broadcast_to(value[:, first + k : first + k + 1], (8, size)) for k in range(8)]

    diagonal = spread_columns(rows[0], 0)
    for home in range(count):
        first = 8 * home
        more = home + 1 < count
        inside = (lane >= first) & (lane < first + 8)
        top = jnp.where(inside, 0.0, rows[home])
        pivots, inverses, ahead, pivot_col = [], [], {}, None
        if more:
            below = spread_columns(rows[home + 1], first)
            coming = spread_columns(rows[home + 1], first + 8)
            below_factors = []
        for step in range(8):
            pivot = spread_row(diagonal[step], step)
            pivot_col = pivot if pivot_col is None else jnp.where(sub == step, pivot, pivot_col)
            inverse = 1.0 / pivot
            inverses.append(inverse)
            factor = jnp.where(sub > step, diagonal[step] * inverse, 0.0)
            for k in range(step + 1, 8):
                ahead[k, step] = spread_row(diagonal[k], step)
                diagonal[k] = diagonal[k] - factor * ahead[k, step]
            if more:
                part = below[step] * inverse
                below_factors.append(part)
                for k in range(step + 1, 8):
                    below[k] = below[k] - part * ahead[k, step]
                for k in range(8):
                    coming[k] = coming[k] - part * spread_row(below[step], k)
            row = jnp.where(lane == first + step, 1.0, spread_row(top, step))
            pivots.append(row)
            if step < 7:
                top = top - factor * row
        for at in range(home + 1, count):
            if at == home + 1:
                factors = below_factors
            else:
                columns = spread_columns(rows[at], first)
                factors = []
                for step in range(8):
                    part = columns[step] * inverses[step]
                    factors.append(part)
                    for k in range(step + 1, 8):
                        columns[k] = columns[k] - part * ahead[k, step]
            value = jnp.where(inside, 0.0, rows[at])
            for step in range(8):
                value = value - factors[step] * pivots[step]
            rows[at] = value
        unit = jnp.where(lane < sub + first, top, 0.0) + jnp.where(lane == sub + first, 1.0, 0.0)
        result.append(unit * lax.rsqrt(pivot_col))
        if more:
            diagonal = coming
        yield


def halved_steps(block, result):
    half = block.shape[0] // 2
    upper, lower = [], []
    yield from factor_steps(block[:half, :half], upper)
    upper = jnp.concatenate(upper, axis=0)
    joint = lax.dot_general(block[half:, :half], upper, NT, precision=HIGH, preferred_element_type=F32)
    rest = lax.dot_general(joint, joint, NT, precision=HIGH, preferred_element_type=F32)
    joint = jnp.dot(joint, upper, precision=HIGH, preferred_element_type=F32)
    yield from factor_steps(block[half:, half:] - rest, lower)
    lower = jnp.concatenate(lower, axis=0)
    joint = jnp.dot(lower, joint, precision=HIGH, preferred_element_type=F32)
    result.append(jnp.concatenate([upper, jnp.zeros_like(upper)], axis=1))
    result.append(jnp.concatenate([-joint, lower], axis=1))


def stacked(value):
    high, low = split2(value)
    return jnp.concatenate(
        [jnp.concatenate([high, high], axis=1), jnp.concatenate([low, low], axis=1)], axis=0
    )


def panel_kernel(
    rounds_ref, aux_ref, table_ref, near_ref, far_ref, more_hbm, feat_hbm, prev_hbm,
    new_hbm, resid_ref, part_ref,
    more_ref, feat_ref, prev_ref, cols_ref, squares_ref,
    more_sem, in_sems, out_sems, *, tile, chunk,
):
    feat, points = feat_ref.shape
    width = prev_ref.shape[1]
    size = aux_ref.shape[1]
    chunks = points // chunk

    def incoming(at):
        here = pl.ds(at * chunk, chunk)
        return (
            pltpu.make_async_copy(feat_hbm.at[:, here], feat_ref.at[:, here], in_sems.at[0, at]),
            pltpu.make_async_copy(prev_hbm.at[here, :], prev_ref.at[here, :], in_sems.at[1, at]),
        )

    def outgoing(at):
        here = pl.ds(at * chunk, chunk)
        return pltpu.make_async_copy(cols_ref.at[here, :], new_hbm.at[here, :], out_sems.at[at])

    for at in range(chunks):
        for copy in incoming(at):
            copy.start()

    @pl.when(rounds_ref[0] < ROUNDS)
    def _():
        copy = pltpu.make_async_copy(more_hbm, more_ref, more_sem)
        copy.start()
        copy.wait()

    @pl.when(rounds_ref[0] >= ROUNDS)
    def _():
        more_ref[...] = jnp.zeros_like(more_ref)

    mine = aux_ref[0:1, :]
    scales_row = aux_ref[1:2, :feat]
    noise = aux_ref[2:3, :]
    scales_col = jnp.broadcast_to(aux_ref[1:2, :], (8, size)).T[:feat, :1]
    core = lax.rem(lax.axis_index("rows"), 2)
    rows = unpack(table_ref[...], near_ref[...], far_ref[...], core) + more_ref[...]
    piv_x = rows[:, :feat]
    piv_f = rows[:, 128:]
    piv_s = piv_x * scales_row
    piv_sq = jnp.sum(piv_s * piv_x, axis=1, keepdims=True)
    pad = jnp.zeros((size, 128 - feat), F32)
    lane = lax.broadcasted_iota(jnp.int32, (size, 128), 1)
    piv_left = jnp.concatenate([piv_x, pad], axis=1)
    piv_left = jnp.where(lane == feat, piv_sq, jnp.where(lane == feat + 1, 1.0, piv_left))
    piv_right = jnp.concatenate([piv_s, pad], axis=1)
    piv_right = jnp.where(lane == feat, -0.5, jnp.where(lane == feat + 1, -0.5 * piv_sq, piv_right))

    fac_rhs = stacked(piv_f)
    x_high, x_mid, x_low = split3(piv_right)
    x_rhs = jnp.concatenate(
        [jnp.concatenate([x_high, x_high], axis=1), jnp.concatenate([x_mid, x_mid], axis=1)], axis=0
    )
    x_rest = jnp.concatenate([x_low, x_high], axis=1)

    def kernel_of(left):
        high, mid, low_part = split3(left)
        two = lax.dot_general(jnp.concatenate([high, mid], axis=1), x_rhs, NT, preferred_element_type=F32)
        rest = lax.dot_general(jnp.concatenate([high, low_part], axis=1), x_rest, NT, preferred_element_type=F32)
        return jnp.exp(two[:, :size] + (two[:, size:] + rest))

    def earlier_of(fac):
        both = lax.dot_general(
            jnp.concatenate(split2(fac), axis=1), fac_rhs, NT, preferred_element_type=F32
        )
        return both[:, :size] + both[:, size:]

    row_id = lax.broadcasted_iota(jnp.int32, (size, size), 0)
    col_id = lax.broadcasted_iota(jnp.int32, (size, size), 1)
    block = kernel_of(piv_left) + jnp.where(row_id == col_id, noise, 0.0) - earlier_of(piv_f)
    inverse_rows = []
    steps = halved_steps(block, inverse_rows)

    sub = lax.broadcasted_iota(jnp.int32, (8, tile), 0)
    ids = lax.broadcasted_iota(jnp.int32, (tile, size), 0).astype(F32)

    def columns(base):
        here = pl.ds(base, tile)
        xt = feat_ref[:, here]
        length = jnp.sum(xt * xt * scales_col, axis=0, keepdims=True)
        extra = jnp.where(sub == 0, length, jnp.where(sub == 1, 1.0, 0.0))
        left = jnp.concatenate([xt, extra, jnp.zeros((128 - feat - 8, tile), F32)], axis=0).T
        kern = kernel_of(left) + jnp.where(ids == mine - base, noise, 0.0)
        fac = prev_ref[here, :]
        cols_ref[here, :] = kern - earlier_of(fac)
        total = fac[:, :128] * fac[:, :128]
        for start in range(128, width, 128):
            total = total + fac[:, start : start + 128] * fac[:, start : start + 128]
        squares_ref[here, :] = total

    for _ in range(5):
        next(steps, None)
    done = 0
    for at in range(points // tile):
        if at in (0, 6):
            for part in range({0: 3, 6: 5}[at]):
                for copy in incoming(done):
                    copy.wait()
                done += 1
        columns(at * tile)
        next(steps, None)
    for _ in steps:
        pass

    inv_rhs = stacked(jnp.concatenate(inverse_rows, axis=0))
    total = jnp.zeros((1, 128), F32)
    for at in range(chunks):
        for inner in range(chunk // tile):
            base = at * chunk + inner * tile
            here = pl.ds(base, tile)
            high, low_part = split2(cols_ref[here, :])
            both = lax.dot_general(
                jnp.concatenate([high, low_part], axis=1), inv_rhs, NT, preferred_element_type=F32
            )
            new = both[:, :size] + both[:, size:]
            cols_ref[here, :] = new
            gone = squares_ref[here, :] + new * new
            for sub_at in range(tile // 128):
                flipped = gone[sub_at * 128 : (sub_at + 1) * 128, :].T
                row = 1.0 + noise - jnp.sum(flipped, axis=0, keepdims=True)
                resid_ref[pl.ds(base // 128 + sub_at, 1), :] = row
                total = total + row
        outgoing(at).start()
    part_ref[...] = jnp.broadcast_to(jnp.sum(total, axis=1, keepdims=True), part_ref.shape)
    for at in range(chunks):
        outgoing(at).wait()


def run_panel(devices, rounds, aux, table, near, far, more, feat_t, prev):
    feat, points = feat_t.shape
    width = prev.shape[1]
    size = aux.shape[1]
    chunk = 512
    return pl.pallas_call(
        functools.partial(panel_kernel, tile=256, chunk=chunk),
        out_shape=(
            jax.ShapeDtypeStruct((points, size), F32),
            jax.ShapeDtypeStruct((points // 128, 128), F32),
            jax.ShapeDtypeStruct((devices, 128), F32),
        ),
        in_specs=[SMEM] + [VMEM] * 4 + [ANY] * 3,
        out_specs=(ANY, VMEM, VMEM),
        scratch_shapes=[
            pltpu.VMEM(more.shape, F32),
            pltpu.VMEM((feat, points), F32),
            pltpu.VMEM((points, width), F32),
            pltpu.VMEM((points, size), F32),
            pltpu.VMEM((points, 128), F32),
            pltpu.SemaphoreType.DMA,
            pltpu.SemaphoreType.DMA((2, points // chunk)),
            pltpu.SemaphoreType.DMA((points // chunk,)),
        ],
        compiler_params=pltpu.CompilerParams(vmem_limit_bytes=PANEL),
        name="panel",
    )(rounds, aux, table, near, far, more, feat_t, prev)


def local(devices, features, prev_factors, inv_scales, noise, pivot_owner, pivot_local):
    points, feat = features.shape
    feat_t = features.T
    layer = groups_of(devices, ((1, 2), (16, 16)))
    column = groups_of(devices, ((2, LAYERS),))
    cores = [(at, at ^ 1) for at in range(devices)]

    def fetch(at_round):
        picked = run_pick(at_round, pivot_owner, pivot_local, feat_t, prev_factors)
        landed = exchange(picked.reshape(32, RANKS, 256), layer)
        pack_table, table, aux, more, rounds = run_table(
            at_round, noise, pivot_owner, pivot_local, inv_scales.reshape(1, feat)
        )
        packed = run_pack(pack_table, landed.reshape(32 * RANKS, 256))
        near = exchange(packed, column)
        return table, near, lax.ppermute(near, "rows", cores), aux, more, rounds

    def again(carry):
        at_round, more = carry
        table, near, far, _, _, coming = fetch(at_round)
        return coming, more + unpack(table, near, far, lax.rem(lax.axis_index("rows"), 2))

    table, near, far, aux, more, rounds = fetch(jnp.zeros((1,), jnp.int32))
    _, more = lax.while_loop(lambda carry: carry[0][0] < ROUNDS, again, (rounds, more))
    new_factors, resid, part = run_panel(devices, rounds, aux, table, near, far, more, feat_t, prev_factors)
    sums = exchange(part.reshape(devices, 1, 128), None)
    trace = jnp.sum(sums[:, 0, 0]).reshape(1)
    return new_factors, resid.reshape(points), trace


def solution(mesh):
    placed = (P("rows", None), P("rows", None), P(), P(), P(), P())
    return jax.shard_map(
        functools.partial(local, mesh.shape["rows"]),
        mesh=mesh,
        in_specs=placed,
        out_specs=(P("rows", None), P("rows"), P()),
        check_vma=False,
    )
```
